128 devices in a mesh: row: 8 (over z_hi, x), col: 16 (over z_lo, y, core).
Axes of the slice: x: 4, y: 4, z: 4 (z_hi: 2, z_lo: 2; z = z_hi * 2 + z_lo), core: 2. Of those that a mesh axis runs over, the one named last changes fastest.
Arguments:
- samples: bfloat16 [262144, 2048], P(('row', 'col')), may hold values from -6 to 6
- prev_factor: float32 [262144, 992], P(('row', 'col')), may hold values from -0.03 to 0.03
- pivots: int32 [32], replicated, may hold values from 0 to 262143, as said below
- inv_diag: float32 [262144], P(('row', 'col')), may hold values from 0.1 to 3
- rhs: float32 [262144], P(('row', 'col')), may hold values from -6 to 6
Outputs:
- new_cols: float32 [262144, 32], P(('row', 'col'))
- solution: float32 [262144], P(('row', 'col'))
The draws below stay inside these ranges and needn't reach their ends.
Inputs may be any that keep to these rules, and one draw needn't show every extreme that they name: `pivots`: 32 distinct sample indices.
All inputs are finite; a program needn't handle non-finite values.
Results may differ from the reference program's by a relative error of at most 0.0003.
Values sent between devices are 32-bit elements; how exact they have to be, the bound alone decides.
No kernel may reach another device: no remote copies, remote signals or barrier semaphores. Data moves between devices by JAX's collectives and lax.ppermute only.
A program may use at most 128 MiB of HBM per device.

```python
import math
import jax
import jax.numpy as jnp
from jax import lax

ROWS_DEV = 2048
FEAT = 2048
PREV = 992
PANEL = 32
RANK = 1024
SAMPLES = 262144


def draw_pivots(key, part):
    key = jax.random.fold_in(key, 11)
    order = jax.random.permutation(key, jnp.arange(SAMPLES, dtype=jnp.int32))
    return order[:PANEL].astype(jnp.int32)


def draw_prev_factor(key, part):
    key = jax.random.fold_in(key, 23)
    subkeys = jax.random.split(key, 6)
    latent = jax.random.normal(subkeys[0], (SAMPLES, 3), jnp.float32)
    col_scale = jnp.exp(jax.random.uniform(subkeys[5], (PREV,), jnp.float32, -2.5, 0.0))
    frequency = jax.random.uniform(subkeys[1], (3, PREV), jnp.float32, -3.0, 3.0)
    phases = jax.random.uniform(subkeys[2], (PREV,), jnp.float32, -math.pi, math.pi)
    col_means = jax.random.uniform(subkeys[3], (PREV,), jnp.float32, -0.4, 0.4)
    jitter = jax.random.uniform(subkeys[4], (SAMPLES, PREV), jnp.float32, -1.0, 1.0)
    argument = latent[:, 0:1] * frequency[0] + latent[:, 1:2] * frequency[1] + latent[:, 2:3] * frequency[2] + phases
    values = 0.017 * (jnp.cos(argument) + col_means + 0.3 * jitter)
    return (values * col_scale).astype(jnp.float32)


def block_levels(rng, extent, cuts, smallest, largest):
    def one(dim, blocks):
        draws = jax.random.uniform(jax.random.fold_in(jax.random.fold_in(rng, 6), dim), (blocks,), jnp.float32, smallest / len(cuts), largest / len(cuts))
        return jnp.repeat(jnp.exp(draws), extent[dim] // blocks).reshape((-1,) + (1,) * (len(extent) - dim - 1))

    level = one(*cuts[0])
    for cut in cuts[1:]:
        level = level * one(*cut)
    return level


def noise(stream_key, dims, deviation, reach, pieces=(), kind=jnp.bfloat16):
    result = jax.random.normal(stream_key, dims, jnp.float32) * deviation
    if len(pieces) > 0:
        result = block_levels(stream_key, dims, pieces, -0.22, 0.18) * result
    return jnp.clip(result, min=-reach, max=reach).astype(kind)


def setup_inputs(seed: int = 0) -> dict:
    key_list = jax.random.split(jax.random.key(seed), 6)
    return {
        "samples": noise(key_list[0], (SAMPLES, FEAT), 1.0, 6.0, ((0, 128),)),
        "prev_factor": draw_prev_factor(jax.random.fold_in(key_list[5], 71), 0),
        "pivots": draw_pivots(jax.random.fold_in(key_list[5], 71), 0),
        "inv_diag": jnp.clip(jnp.exp(math.log(3.0) - 3.4011974 * jax.random.uniform(key_list[3], (SAMPLES,), jnp.float32) ** block_levels(key_list[3], (SAMPLES,), ((0, 128),), -0.2, 0.2)), 0.1, 3.0),
        "rhs": noise(key_list[4], (SAMPLES,), 1.0, 6.0, ((0, 128),), jnp.float32),
    }


def reference(samples, prev_factor, pivots, inv_diag, rhs):
    upcast = samples.astype(jnp.float32)
    sqnorm = jnp.sum(upcast * upcast, axis=1)
    picked = samples[pivots]
    cross = jnp.dot(samples.astype(jnp.float32), picked.T.astype(jnp.float32), preferred_element_type=jnp.float32)
    dist = jnp.maximum(sqnorm[:, None] + sqnorm[pivots][None, :] - 2.0 * cross, 0.0)
    kcols = jnp.exp(-(2.0 / FEAT) * dist)
    resid = kcols - jnp.dot(prev_factor, prev_factor[pivots].T, precision=lax.Precision.HIGHEST)
    chol = jnp.linalg.cholesky(resid[pivots])
    new_cols = lax.linalg.triangular_solve(chol, resid, left_side=False, lower=True, transpose_a=True)
    factor = jnp.concatenate([prev_factor, new_cols], axis=1)
    blocks = factor.reshape(SAMPLES // ROWS_DEV, ROWS_DEV, RANK)
    dblocks = inv_diag.reshape(SAMPLES // ROWS_DEV, ROWS_DEV)
    weighted_rhs = inv_diag * rhs
    wblocks = weighted_rhs.reshape(SAMPLES // ROWS_DEV, ROWS_DEV)

    def accumulate(carry, item):
        block, dvals, wvals = item
        gram = carry[0] + jnp.dot(block.T, dvals[:, None] * block, precision=lax.Precision.HIGHEST)
        moment = carry[1] + jnp.dot(block.T, wvals, precision=lax.Precision.HIGHEST)
        return ((gram, moment), None)
    start = (jnp.zeros((RANK, RANK), jnp.float32), jnp.zeros((RANK,), jnp.float32))
    (gram, moment), unused = lax.scan(accumulate, start, (blocks, dblocks, wblocks))
    system = jnp.eye(RANK, dtype=jnp.float32) + gram
    lower = jnp.linalg.cholesky(system)
    forward = lax.linalg.triangular_solve(lower, moment[:, None], left_side=True, lower=True)
    weights = lax.linalg.triangular_solve(lower, forward, left_side=True, lower=True, transpose_a=True)[:, 0]
    solution = weighted_rhs - inv_diag * jnp.dot(factor, weights, precision=lax.Precision.HIGHEST)
    return (new_cols, solution)
```

```python
import functools

import jax
import jax.numpy as jnp
from jax import lax
from jax.experimental import pallas as pl
from jax.experimental.pallas import tpu as pltpu
from jax.sharding import PartitionSpec as P

FEAT = 2048
PREV = 992
PANEL = 32
RANK = 1024
ROWS = 2048
LANES = 128
NB = RANK // LANES
GRAM_ROWS = sum((NB - j) * LANES for j in range(NB))
PICK_ROWS = PANEL * (FEAT + RANK) // LANES
SEND_ROWS = 6144
EXT = 40
EXT_ROWS = 512
HIGHEST = lax.Precision.HIGHEST
F32 = jnp.float32
BF16 = jnp.bfloat16
AXES = ("row", "col")


def split(x):
    high = x.astype(BF16)
    return high, (x - high.astype(F32)).astype(BF16)


def mm(a, b, dims, precision=None):
    return lax.dot_general(a, b, (dims, ((), ())), precision=precision, preferred_element_type=F32)


NN = ((1,), (0,))
NT = ((1,), (1,))
TN = ((0,), (0,))


def column(row):
    return jnp.broadcast_to(row, (LANES, LANES)).T


GRAM_TILE = 512


def gram_kernel(pivots_ref, base_ref, diag_ref, samples_ref, prev_any, prev_ref, out_ref, y_ref, acc_ref, srow_ref, frow_ref, sem):
    step = pl.program_id(0)
    base = base_ref[0]

    def row_copies(p):
        place = pivots_ref[p] - base
        s0 = pl.multiple_of(place // 16 * 16, 16)
        f0 = pl.multiple_of(place // 8 * 8, 8)
        return (
            place,
            pltpu.make_async_copy(samples_ref.at[pl.ds(s0, 16)], srow_ref.at[p], sem.at[0, p]),
            pltpu.make_async_copy(prev_any.at[pl.ds(f0, 8)], frow_ref.at[p], sem.at[1, p]),
        )

    def owned(p):
        place = pivots_ref[p] - base
        return (place >= 0) & (place < ROWS)

    @pl.when(step == 0)
    def _():
        acc_ref[...] = jnp.zeros_like(acc_ref)
        y_ref[:, PREV:] = jnp.zeros((GRAM_TILE, RANK - PREV), F32)
        out_ref[GRAM_ROWS:, :] = jnp.zeros((SEND_ROWS - GRAM_ROWS, LANES), F32)

        def start(p, carry):
            @pl.when(owned(p))
            def _():
                place, a, b = row_copies(p)
                a.start()
                b.start()

            return carry

        lax.fori_loop(0, PANEL, start, 0)

    for c in range(GRAM_TILE // LANES):
        scale = jnp.sqrt(column(diag_ref[pl.ds(step * (GRAM_TILE // LANES) + c, 1), :]))[:, :1]
        y_ref[c * LANES : (c + 1) * LANES, :PREV] = prev_ref[c * LANES : (c + 1) * LANES, :] * scale
    high, low = split(y_ref[...])
    for j in range(4):
        left_h = high[:, 256 * j :]
        left_l = low[:, 256 * j :]
        right_h = high[:, 256 * j : 256 * j + 256]
        right_l = low[:, 256 * j : 256 * j + 256]
        total = mm(left_h, right_h, TN) + mm(left_h, right_l, TN) + mm(left_l, right_h, TN)
        at = 1024 * j - 128 * j * (j - 1)
        acc_ref[at : at + RANK - 256 * j, :] += total

    @pl.when(step == 1)
    def _():
        def finish(p, carry):
            @pl.when(owned(p))
            def _():
                place, a, b = row_copies(p)
                a.wait()
                b.wait()
                sub = lax.broadcasted_iota(jnp.int32, (16, FEAT), 0)
                srow = jnp.sum(jnp.where(sub == place % 16, srow_ref[p].astype(F32), 0.0), axis=0, keepdims=True)
                sub = lax.broadcasted_iota(jnp.int32, (8, PREV), 0)
                frow = jnp.sum(jnp.where(sub == place % 8, frow_ref[p], 0.0), axis=0, keepdims=True)
                for c in range(FEAT // LANES):
                    out_ref[pl.ds(GRAM_ROWS + c * PANEL + p, 1), :] = srow[:, c * LANES : (c + 1) * LANES]
                at = GRAM_ROWS + PANEL * FEAT // LANES
                for c in range(PREV // LANES):
                    out_ref[pl.ds(at + c * PANEL + p, 1), :] = frow[:, c * LANES : (c + 1) * LANES]
                rest = PREV % LANES
                out_ref[pl.ds(at + (NB - 1) * PANEL + p, 1), :rest] = frow[:, PREV - rest :]

            return carry

        lax.fori_loop(0, PANEL, finish, 0)

    @pl.when(step == ROWS // GRAM_TILE - 1)
    def _():
        to = 0
        for j in range(NB):
            big = j // 2
            at = 1024 * big - 128 * big * (big - 1) + (j % 2) * LANES
            n = RANK - LANES * j
            lane = (j % 2) * LANES
            out_ref[to : to + n, :] = acc_ref[at : at + n, lane : lane + LANES]
            to += n


def gram(samples, prev_factor, pivots, inv_diag, base):
    big_rows = sum(RANK - 256 * j for j in range(4))
    return pl.pallas_call(
        gram_kernel,
        grid=(ROWS // GRAM_TILE,),
        out_shape=jax.ShapeDtypeStruct((SEND_ROWS, LANES), F32),
        in_specs=[
            pl.BlockSpec(memory_space=pltpu.SMEM),
            pl.BlockSpec(memory_space=pltpu.SMEM),
            pl.BlockSpec((ROWS // LANES, LANES), lambda i: (0, 0)),
            pl.BlockSpec(memory_space=pl.ANY),
            pl.BlockSpec(memory_space=pl.ANY),
            pl.BlockSpec((GRAM_TILE, PREV), lambda i: (i, 0)),
        ],
        out_specs=pl.BlockSpec((SEND_ROWS, LANES), lambda i: (0, 0)),
        scratch_shapes=[
            pltpu.VMEM((GRAM_TILE, RANK), F32),
            pltpu.VMEM((big_rows, 256), F32),
            pltpu.VMEM((PANEL, 16, FEAT), BF16),
            pltpu.VMEM((PANEL, 8, PREV), F32),
            pltpu.SemaphoreType.DMA((2, PANEL)),
        ],
        compiler_params=pltpu.CompilerParams(vmem_limit_bytes=50 * 2**20),
        cost_estimate=pl.CostEstimate(flops=3 * 2 * ROWS * RANK * 640, bytes_accessed=ROWS * PREV * 4 + SEND_ROWS * 512, transcendentals=0),
        name="gram",
    )(pivots, base, inv_diag, samples, prev_factor, prev_factor)


PANEL_TILE = 256


def panel_kernel(picks_ref, diag_ref, rhs_ref, samples_ref, prev_ref, new_ref, ext_ref, picked_ref, ph_ref, pl_ref, norm_ref, inv_ref, y_ref, acc_ref):
    step = pl.program_id(0)
    nfeat = FEAT // LANES

    @pl.when(step == 0)
    def _():
        acc_ref[...] = jnp.zeros_like(acc_ref)
        y_ref[:, PREV:] = jnp.zeros((PANEL_TILE, RANK - PREV), F32)
        picked = jnp.concatenate([picks_ref[c * PANEL : (c + 1) * PANEL, :] for c in range(nfeat)], axis=1)
        pfac = jnp.concatenate([picks_ref[(nfeat + c) * PANEL : (nfeat + c + 1) * PANEL, :] for c in range(NB)], axis=1)
        picked16 = picked.astype(BF16)
        picked_ref[...] = picked16
        high, low = split(pfac)
        ph_ref[...] = high
        pl_ref[...] = low
        square = picked * picked
        norm_row = mm(jnp.ones((8, FEAT), F32), square, NT, HIGHEST)[:1]
        norm_col = jnp.sum(square, axis=1, keepdims=True)
        norm_ref[...] = jnp.broadcast_to(norm_row, (8, PANEL))
        cross = mm(picked16, picked16, NT)
        dist = jnp.maximum(norm_col + norm_row - 2.0 * cross, 0.0)
        a = jnp.exp(-(2.0 / FEAT) * dist) - mm(pfac, pfac, NT, HIGHEST)
        sub = lax.broadcasted_iota(jnp.int32, (PANEL, PANEL), 0)
        lane = lax.broadcasted_iota(jnp.int32, (PANEL, PANEL), 1)
        b = jnp.where(sub == lane, 1.0, 0.0)
        for k in range(PANEL - 1):
            factor = jnp.where(sub > k, a[:, k : k + 1] / a[k : k + 1, k : k + 1], 0.0)
            a, b = a - factor * a[k : k + 1, :], b - factor * b[k : k + 1, :]
        pivot = jnp.sum(jnp.where(sub == lane, a, 0.0), axis=1, keepdims=True)
        inv_ref[...] = b / jnp.sqrt(pivot)

    tile = samples_ref[...]
    wide = tile.astype(F32)
    norm = jnp.sum(wide * wide, axis=1, keepdims=True)
    cross = mm(tile, picked_ref[...], NT)
    dist = jnp.maximum(norm + norm_ref[:1, :] - 2.0 * cross, 0.0)
    y_ref[:, :PREV] = prev_ref[...]
    lane = lax.broadcasted_iota(jnp.int32, (PANEL_TILE, LANES), 1)
    last = y_ref[:, RANK - LANES :]
    y_ref[:, RANK - LANES :] = jnp.where(lane < PREV % LANES, last, 0.0)
    high, low = split(y_ref[...])
    inner = mm(high, ph_ref[...], NT) + (mm(high, pl_ref[...], NT) + mm(low, ph_ref[...], NT))
    resid = jnp.exp(-(2.0 / FEAT) * dist) - inner
    inverse = inv_ref[...]
    new_ref[...] = mm(resid, inverse, NT, HIGHEST)
    zeros = jnp.zeros((LANES - PANEL, PANEL), F32)
    new_last = mm(resid, jnp.concatenate([zeros, inverse], axis=0), NT, HIGHEST)
    new_first = mm(resid, jnp.concatenate([inverse, zeros], axis=0), NT, HIGHEST)
    y_ref[:, RANK - LANES :] = y_ref[:, RANK - LANES :] + new_last
    chunks = range(PANEL_TILE // LANES)
    rows = [pl.ds(step * (PANEL_TILE // LANES) + c, 1) for c in chunks]
    dcol = jnp.concatenate([column(diag_ref[r, :]) for r in rows], axis=0)
    rcol = jnp.concatenate([column(rhs_ref[r, :]) for r in rows], axis=0)
    x = dcol * jnp.where(lane == PANEL, rcol, new_first)
    xh, xl = split(x)
    high, low = split(y_ref[...])
    total = mm(xh, high, TN) + (mm(xl, high, TN) + mm(xh, low, TN))
    acc_ref[...] += total[:EXT]

    @pl.when(step == ROWS // PANEL_TILE - 1)
    def _():
        for c in range(NB):
            ext_ref[EXT * c : EXT * (c + 1), :] = acc_ref[:, c * LANES : (c + 1) * LANES]
        ext_ref[EXT * NB :, :] = jnp.zeros((EXT_ROWS - EXT * NB, LANES), F32)


def panel(picks, inv_diag, rhs, samples, prev_factor):
    whole = lambda i: (0, 0)
    return pl.pallas_call(
        panel_kernel,
        grid=(ROWS // PANEL_TILE,),
        out_shape=(jax.ShapeDtypeStruct((ROWS, PANEL), F32), jax.ShapeDtypeStruct((EXT_ROWS, LANES), F32)),
        in_specs=[
            pl.BlockSpec((PICK_ROWS, LANES), whole),
            pl.BlockSpec((ROWS // LANES, LANES), whole),
            pl.BlockSpec((ROWS // LANES, LANES), whole),
            pl.BlockSpec((PANEL_TILE, FEAT), lambda i: (i, 0)),
            pl.BlockSpec((PANEL_TILE, PREV), lambda i: (i, 0)),
        ],
        out_specs=(pl.BlockSpec((PANEL_TILE, PANEL), lambda i: (i, 0)), pl.BlockSpec((EXT_ROWS, LANES), whole)),
        scratch_shapes=[
            pltpu.VMEM((PANEL, FEAT), BF16),
            pltpu.VMEM((PANEL, RANK), BF16),
            pltpu.VMEM((PANEL, RANK), BF16),
            pltpu.VMEM((8, PANEL), F32),
            pltpu.VMEM((PANEL, PANEL), F32),
            pltpu.VMEM((PANEL_TILE, RANK), F32),
            pltpu.VMEM((EXT, RANK), F32),
        ],
        compiler_params=pltpu.CompilerParams(vmem_limit_bytes=50 * 2**20),
        cost_estimate=pl.CostEstimate(flops=2 * ROWS * RANK * 1000, bytes_accessed=ROWS * (FEAT * 2 + PREV * 4), transcendentals=0),
        name="panel",
    )(picks, inv_diag, rhs, samples, prev_factor)


def inverse8(cols):
    sub = lax.broadcasted_iota(jnp.int32, (8, LANES), 0)

    def row(x, r):
        return jnp.broadcast_to(x[r : r + 1, :], (8, LANES))

    cols = list(cols)
    for k in range(0, 8, 2):
        a, b, c = row(cols[k], k), row(cols[k + 1], k), row(cols[k + 1], k + 1)
        scale = 1.0 / (a * c - b * b)
        ia, ib, ic = c * scale, -b * scale, a * scale
        ua = cols[k] * ia + cols[k + 1] * ib
        ub = cols[k] * ib + cols[k + 1] * ic
        keep = (sub != k) & (sub != k + 1)
        first = sub == k
        for m in range(8):
            if m in (k, k + 1):
                continue
            x, y = row(cols[m], k), row(cols[m], k + 1)
            cols[m] = jnp.where(keep, cols[m] - (ua * x + ub * y), jnp.where(first, ia * x + ib * y, ib * x + ic * y))
        cols[k] = jnp.where(keep, -ua, jnp.where(first, ia, ib))
        cols[k + 1] = jnp.where(keep, -ub, jnp.where(first, ib, ic))
    return cols


def tree(terms):
    while len(terms) > 1:
        terms = [a + b for a, b in zip(terms[::2], terms[1::2])]
    return terms[0]


def inverse128(rows):
    lane = lax.broadcasted_iota(jnp.int32, (8, LANES), 1)
    sub = lax.broadcasted_iota(jnp.int32, (8, LANES), 0)
    rows = list(rows)
    n = len(rows)

    def spread(x, at):
        return jnp.broadcast_to(x[:, at : at + 1], (8, LANES))

    for p in range(n):
        inside = (lane >= 8 * p) & (lane < 8 * p + 8)
        cols = inverse8([spread(rows[p], 8 * p + j) for j in range(8)])
        own = jnp.where(inside, jnp.where(lane == sub + 8 * p, 1.0, 0.0), rows[p])
        pivot = tree([cols[j] * jnp.broadcast_to(own[j : j + 1, :], (8, LANES)) for j in range(8)])
        spread_rows = [jnp.broadcast_to(pivot[j : j + 1, :], (8, LANES)) for j in range(8)]
        rows[p] = pivot
        for step in range(1, n):
            q = (p + step) % n
            update = tree([spread(rows[q], 8 * p + j) * spread_rows[j] for j in range(8)])
            rows[q] = jnp.where(inside, 0.0, rows[q]) - update
    return rows


EXTRA = EXT - PANEL
SOLVE_AT = [sum((NB - m) * LANES + EXTRA for m in range(j)) for j in range(NB + 1)]


def solve_kernel(gram_ref, ext_ref, w_ref, a_ref, t_ref):
    lane = lax.broadcasted_iota(jnp.int32, (LANES, LANES), 1)
    sub = lax.broadcasted_iota(jnp.int32, (LANES, LANES), 0)
    at = 0
    for j in range(NB):
        n = (NB - j) * LANES
        to = SOLVE_AT[j]
        a_ref[to : to + n - PANEL, :] = gram_ref[at : at + n - PANEL, :]
        a_ref[to + n - PANEL : to + n + EXTRA, :] = ext_ref[EXT * j : EXT * (j + 1), :]
        at += n
    to = SOLVE_AT[NB - 1]
    last = a_ref[to : to + LANES, :]
    a_ref[to : to + LANES, :] = jnp.where((lane >= PREV % LANES) & (sub < PREV % LANES), last.T, last)
    for k in range(NB):
        to = SOLVE_AT[k]
        a_ref[to : to + LANES, :] += jnp.where(lane == sub, 1.0, 0.0)
        block = inverse128([a_ref[to + 8 * i : to + 8 * i + 8, :] for i in range(LANES // 8)])
        n = (NB - k - 1) * LANES + EXTRA
        below = a_ref[to + LANES : to + LANES + n, :]
        times = mm(below, jnp.concatenate(block, axis=0), NN, HIGHEST)
        t_ref[to : to + n, :] = times
        for j in range(k + 1, NB):
            r = (j - k - 1) * LANES
            a_ref[SOLVE_AT[j] : SOLVE_AT[j] + n - r, :] -= mm(times[r:], below[r : r + LANES], NT, HIGHEST)
    weights = [None] * NB
    for k in reversed(range(NB)):
        n = (NB - k - 1) * LANES
        to = SOLVE_AT[k]
        value = t_ref[to + n : to + n + EXTRA, :]
        for i in range(k + 1, NB):
            r = to + (i - k - 1) * LANES
            value = value - mm(weights[i], t_ref[r : r + LANES, :], NN, HIGHEST)
        weights[k] = value
    for k in range(NB):
        w_ref[:, LANES * k : LANES * (k + 1)] = weights[k]


def solve(summed, ext):
    return pl.pallas_call(
        solve_kernel,
        grid=(1,),
        out_shape=jax.ShapeDtypeStruct((EXTRA, RANK), F32),
        in_specs=[pl.BlockSpec((GRAM_ROWS, LANES), lambda i: (0, 0)), pl.BlockSpec((EXT_ROWS, LANES), lambda i: (0, 0))],
        out_specs=pl.BlockSpec((EXTRA, RANK), lambda i: (0, 0)),
        scratch_shapes=[pltpu.VMEM((SOLVE_AT[NB], LANES), F32), pltpu.VMEM((SOLVE_AT[NB], LANES), F32)],
        compiler_params=pltpu.CompilerParams(vmem_limit_bytes=50 * 2**20),
        name="solve",
    )(summed, ext)


FINAL_TILE = 512


def final_kernel(w_ref, diag_ref, rhs_ref, prev_ref, new_ref, out_ref, y_ref):
    y_ref[:, RANK - LANES :] = jnp.zeros((FINAL_TILE, LANES), F32)
    y_ref[:, :PREV] = prev_ref[...]
    wh, wl = split(w_ref[...])
    yh, yl = split(y_ref[...])
    nh, nl = split(new_ref[...])
    th, tl = wh[:, PREV:], wl[:, PREV:]
    fw = mm(wh, yh, NT) + (mm(wl, yh, NT) + mm(wh, yl, NT))
    fw = fw + (mm(th, nh, NT) + (mm(tl, nh, NT) + mm(th, nl, NT)))
    out_ref[...] = diag_ref[...] * rhs_ref[...] - diag_ref[...] * fw[:1, :]


def final(w, inv_diag, rhs, prev_factor, new_cols):
    whole = lambda i: (0, 0)
    vec = pl.BlockSpec((1, FINAL_TILE), lambda i: (0, i))
    return pl.pallas_call(
        final_kernel,
        grid=(ROWS // FINAL_TILE,),
        out_shape=jax.ShapeDtypeStruct((1, ROWS), F32),
        in_specs=[
            pl.BlockSpec((EXTRA, RANK), whole),
            vec,
            vec,
            pl.BlockSpec((FINAL_TILE, PREV), lambda i: (i, 0)),
            pl.BlockSpec((FINAL_TILE, PANEL), lambda i: (i, 0)),
        ],
        out_specs=vec,
        scratch_shapes=[pltpu.VMEM((FINAL_TILE, RANK), F32)],
        compiler_params=pltpu.CompilerParams(vmem_limit_bytes=50 * 2**20),
        name="final",
    )(w, inv_diag, rhs, prev_factor, new_cols)


SAME_CORE = [[i for i in range(128) if i % 2 == core] for core in range(2)]
OTHER_CORE = [(i, i ^ 1) for i in range(128)]


def sum_large(x):
    core = lax.axis_index("col") % 2
    halves = x.reshape(2, 64, x.shape[0] // 128, LANES)
    mine = lax.dynamic_index_in_dim(halves, core, 0, keepdims=False)
    other = lax.dynamic_index_in_dim(halves, 1 - core, 0, keepdims=False)
    mine = mine + lax.ppermute(other, AXES, OTHER_CORE)
    parts = lax.all_to_all(mine, AXES, 0, 0, axis_index_groups=SAME_CORE)
    part = jnp.sum(parts, axis=0)
    mine = lax.all_to_all(jnp.broadcast_to(part, mine.shape), AXES, 0, 0, axis_index_groups=SAME_CORE)
    other = lax.ppermute(mine, AXES, OTHER_CORE)
    mine, other = mine.reshape(-1, LANES), other.reshape(-1, LANES)
    return jnp.where(core == 0, jnp.concatenate([mine, other]), jnp.concatenate([other, mine]))


def sum_small(x):
    parts = lax.all_to_all(x.reshape(128, -1, LANES), AXES, 0, 0)
    part = jnp.sum(parts, axis=0)
    return lax.all_to_all(jnp.broadcast_to(part, parts.shape), AXES, 0, 0).reshape(x.shape)


def on_device(samples, prev_factor, pivots, inv_diag, rhs):
    base = (lax.axis_index(AXES) * ROWS).astype(jnp.int32).reshape(1)
    diag2, rhs2 = inv_diag.reshape(ROWS // LANES, LANES), rhs.reshape(ROWS // LANES, LANES)
    local = gram(samples, prev_factor, pivots, diag2, base)
    summed = sum_large(local)
    picks = summed[GRAM_ROWS : GRAM_ROWS + PICK_ROWS]
    new_cols, ext = panel(picks, diag2, rhs2, samples, prev_factor)
    ext = sum_small(ext)
    w = solve(summed, ext)
    out = final(w, inv_diag.reshape(1, ROWS), rhs.reshape(1, ROWS), prev_factor, new_cols)
    return (new_cols, out.reshape(ROWS))


def solution(mesh):
    return jax.shard_map(
        on_device,
        mesh=mesh,
        in_specs=(
            P(AXES, None),
            P(AXES, None),
            P(),
            P(AXES),
            P(AXES),
        ),
        out_specs=(P(AXES, None), P(AXES)),
        check_vma=False,
    )
```

```python
import functools

import jax
import jax.numpy as jnp
from jax import lax
from jax.experimental import pallas as pl
from jax.experimental.pallas import tpu as pltpu
from jax.sharding import PartitionSpec as P

FEAT = 2048
PREV = 992
PANEL = 32
RANK = 1024
ROWS = 2048
LANES = 128
NB = RANK // LANES
PACKED = [PREV - j * LANES for j in range(NB)]
PACKED_AT = [sum(PACKED[:j]) for j in range(NB + 1)]
GRAM_ROWS = PACKED_AT[NB]
PICK_ROWS = PANEL * (FEAT + RANK) // LANES
SEND_ROWS = GRAM_ROWS + PICK_ROWS
HALF = SEND_ROWS // 2
EXT = 40
EXT_ROWS = 512
HIGHEST = lax.Precision.HIGHEST
F32 = jnp.float32
BF16 = jnp.bfloat16
AXES = ("row", "col")
VMEM_LIMIT = 50 * 2**20


def split(x):
    high = x.astype(BF16)
    return high, (x - high.astype(F32)).astype(BF16)


def mm(a, b, dims, precision=None):
    return lax.dot_general(a, b, (dims, ((), ())), precision=precision, preferred_element_type=F32)


NN = ((1,), (0,))
NT = ((1,), (1,))


def whole(i):
    return (0, 0)


def by_half(start, stop):
    cuts = [start] + [HALF] * (start < HALF < stop) + [stop]
    return [(a // HALF, a % HALF, a - start, b - a) for a, b in zip(cuts, cuts[1:])]


GRAM_TILE = 512


def gram_kernel(pivots_ref, place_ref, diag_ref, samples_ref, prev_ref, keep_ref, send_ref, acc_ref, picks_ref, srow_ref, sem):
    step = pl.program_id(0)
    base = place_ref[0]

    def row_copy(p):
        start = pl.multiple_of((pivots_ref[p] - base) // 16 * 16, 16)
        return pltpu.make_async_copy(samples_ref.at[pl.ds(start, 16)], srow_ref.at[p], sem.at[p])

    def owned(p):
        place = pivots_ref[p] - base
        return (place >= 0) & (place < ROWS)

    @pl.when(step == 0)
    def _():
        acc_ref[...] = jnp.zeros_like(acc_ref)
        picks_ref[...] = jnp.zeros_like(picks_ref)

        def start(p, carry):
            @pl.when(owned(p))
            def _():
                row_copy(p).start()

            return carry

        lax.fori_loop(0, PANEL, start, 0)

    high, low = split(prev_ref[...] * jnp.sqrt(diag_ref[...]))
    at = 0
    for j in range(4):
        first = 256 * j
        wide = min(256, PREV - first)
        mine_h, mine_l = high[first : first + wide], low[first : first + wide]
        total = mm(high[first:], mine_h, NT) + (mm(high[first:], mine_l, NT) + mm(low[first:], mine_h, NT))
        acc_ref[at : at + PREV - first, :wide] += total
        at += PREV - first

    def factor_row(p, carry):
        place = pivots_ref[p] - base

        @pl.when(owned(p) & (place // GRAM_TILE == step))
        def _():
            local = place % GRAM_TILE
            start = pl.multiple_of(local // LANES * LANES, LANES)
            chosen = lax.broadcasted_iota(jnp.int32, (8, LANES), 1) == local % LANES
            row = mm(jnp.where(chosen, 1.0, 0.0), prev_ref[:, pl.ds(start, LANES)], NT, HIGHEST)[:1]
            to = PANEL * FEAT // LANES
            for c in range(NB - 1):
                picks_ref[pl.ds(to + c * PANEL + p, 1), :] = row[:, c * LANES : (c + 1) * LANES]
            picks_ref[pl.ds(to + (NB - 1) * PANEL + p, 1), : PREV % LANES] = row[:, (NB - 1) * LANES :]

        return carry

    lax.fori_loop(0, PANEL, factor_row, 0)

    @pl.when(step == ROWS // GRAM_TILE - 1)
    def _():
        def sample_row(p, carry):
            @pl.when(owned(p))
            def _():
                row_copy(p).wait()
                sub = lax.broadcasted_iota(jnp.int32, (16, FEAT), 0)
                row = jnp.sum(jnp.where(sub == (pivots_ref[p] - base) % 16, srow_ref[p].astype(F32), 0.0), axis=0, keepdims=True)
                for c in range(FEAT // LANES):
                    picks_ref[pl.ds(c * PANEL + p, 1), :] = row[:, c * LANES : (c + 1) * LANES]

            return carry

        lax.fori_loop(0, PANEL, sample_row, 0)

        def write(halves):
            at = 0
            for j in range(NB):
                lane = (j % 2) * LANES
                wide = min(LANES, PREV - j * LANES)
                for half, to, skip, n in by_half(PACKED_AT[j], PACKED_AT[j + 1]):
                    halves[half][to : to + n, :wide] = acc_ref[at + lane + skip : at + lane + skip + n, lane : lane + wide]
                    if wide < LANES:
                        halves[half][to : to + n, wide:] = jnp.zeros((n, LANES - wide), F32)
                at += (PREV - j * LANES + LANES) * (j % 2)
            halves[1][GRAM_ROWS - HALF :, :] = picks_ref[...]

        @pl.when(place_ref[1] == 0)
        def _():
            write((keep_ref, send_ref))

        @pl.when(place_ref[1] == 1)
        def _():
            write((send_ref, keep_ref))


def gram(samples, prev_t, pivots, diag, place):
    half = jax.ShapeDtypeStruct((HALF, LANES), F32)
    return pl.pallas_call(
        gram_kernel,
        grid=(ROWS // GRAM_TILE,),
        out_shape=(half, half),
        in_specs=[
            pl.BlockSpec(memory_space=pltpu.SMEM),
            pl.BlockSpec(memory_space=pltpu.SMEM),
            pl.BlockSpec((1, GRAM_TILE), lambda i: (0, i)),
            pl.BlockSpec(memory_space=pl.ANY),
            pl.BlockSpec((PREV, GRAM_TILE), lambda i: (0, i)),
        ],
        out_specs=(pl.BlockSpec((HALF, LANES), whole), pl.BlockSpec((HALF, LANES), whole)),
        scratch_shapes=[
            pltpu.VMEM((sum(PREV - 256 * j for j in range(4)), 256), F32),
            pltpu.VMEM((PICK_ROWS, LANES), F32),
            pltpu.VMEM((PANEL, 16, FEAT), BF16),
            pltpu.SemaphoreType.DMA((PANEL,)),
        ],
        compiler_params=pltpu.CompilerParams(vmem_limit_bytes=VMEM_LIMIT),
        cost_estimate=pl.CostEstimate(flops=6 * ROWS * RANK * 640, bytes_accessed=ROWS * PREV * 4, transcendentals=0),
        name="gram",
    )(pivots, place, diag, samples, prev_t)


PANEL_TILE = 512


def panel_kernel(place_ref, mine_ref, other_ref, diag_ref, rhs_ref, samples_ref, prev_ref, new_ref, ext_ref, picked_ref, pfac_ref, norm_ref, inv_ref, acc_ref):
    step = pl.program_id(0)
    nfeat = FEAT // LANES

    def prepare(picks_ref):
        def pick(c):
            return picks_ref[GRAM_ROWS - HALF + c * PANEL : GRAM_ROWS - HALF + (c + 1) * PANEL, :]

        acc_ref[...] = jnp.zeros_like(acc_ref)
        picked = jnp.concatenate([pick(c) for c in range(nfeat)], axis=1)
        pfac = jnp.concatenate([pick(nfeat + c) for c in range(NB)], axis=1)[:, :PREV]
        picked16 = picked.astype(BF16)
        picked_ref[...] = picked16
        high, low = split(pfac)
        pfac_ref[:PANEL, :] = high
        pfac_ref[PANEL:, :] = low
        square = picked * picked
        norm_row = mm(jnp.ones((8, FEAT), F32), square, NT, HIGHEST)[:1]
        norm_col = jnp.sum(square, axis=1, keepdims=True)
        norm_ref[...] = jnp.broadcast_to(norm_col, (PANEL, LANES))
        cross = mm(picked16, picked16, NT)
        dist = jnp.maximum(norm_col + norm_row - 2.0 * cross, 0.0)
        a = jnp.exp(-(2.0 / FEAT) * dist) - mm(pfac, pfac, NT, HIGHEST)
        sub = lax.broadcasted_iota(jnp.int32, (PANEL, PANEL), 0)
        lane = lax.broadcasted_iota(jnp.int32, (PANEL, PANEL), 1)
        b = jnp.where(sub == lane, 1.0, 0.0)
        for k in range(PANEL - 1):
            factor = jnp.where(sub > k, a[:, k : k + 1] / a[k : k + 1, k : k + 1], 0.0)
            a, b = a - factor * a[k : k + 1, :], b - factor * b[k : k + 1, :]
        pivot = jnp.sum(jnp.where(sub == lane, a, 0.0), axis=1, keepdims=True)
        inv_ref[...] = b / jnp.sqrt(pivot)

    @pl.when((step == 0) & (place_ref[1] == 1))
    def _():
        prepare(mine_ref)

    @pl.when((step == 0) & (place_ref[1] == 0))
    def _():
        prepare(other_ref)

    tile = samples_ref[...]
    squares = None
    for c in range(nfeat):
        part = tile[:, c * LANES : (c + 1) * LANES].astype(F32)
        squares = part * part if squares is None else squares + part * part
    norm = jnp.concatenate(
        [jnp.sum(squares[c : c + LANES].T, axis=0, keepdims=True) for c in range(0, PANEL_TILE, LANES)], axis=1
    )
    cross = mm(picked_ref[...], tile, NT)
    dist = jnp.maximum(norm + norm_ref[:, :1] - 2.0 * cross, 0.0)
    high, low = split(prev_ref[...])
    both = mm(pfac_ref[...], high, NN)
    inner = both[:PANEL] + (both[PANEL:] + mm(pfac_ref[:PANEL, :], low, NN))
    resid = jnp.exp(-(2.0 / FEAT) * dist) - inner
    new = mm(inv_ref[...], resid, NN, HIGHEST)
    new_ref[...] = new
    sub = lax.broadcasted_iota(jnp.int32, (EXT - PANEL, PANEL_TILE), 0)
    x = diag_ref[...] * jnp.concatenate([new, jnp.where(sub == 0, rhs_ref[...], 0.0)], axis=0)
    x = jnp.concatenate([x, jnp.zeros((48 - EXT, PANEL_TILE), F32)], axis=0)
    xh, xl = split(x)
    nh, nl = split(new)
    high, low = jnp.concatenate([high, nh], axis=0), jnp.concatenate([low, nl], axis=0)
    both = mm(jnp.concatenate([xh, xl], axis=0), high, NT)
    acc_ref[...] += both[:EXT] + (both[48 : 48 + EXT] + mm(xh, low, NT)[:EXT])

    @pl.when(step == ROWS // PANEL_TILE - 1)
    def _():
        for c in range(NB):
            ext_ref[EXT * c : EXT * (c + 1), :] = acc_ref[:, c * LANES : (c + 1) * LANES]
        ext_ref[EXT * NB :, :] = jnp.zeros((EXT_ROWS - EXT * NB, LANES), F32)


def panel(place, mine, other, diag, rhs, samples, prev_t):
    vec = pl.BlockSpec((1, PANEL_TILE), lambda i: (0, i))
    return pl.pallas_call(
        panel_kernel,
        grid=(ROWS // PANEL_TILE,),
        out_shape=(jax.ShapeDtypeStruct((PANEL, ROWS), F32), jax.ShapeDtypeStruct((EXT_ROWS, LANES), F32)),
        in_specs=[
            pl.BlockSpec(memory_space=pltpu.SMEM),
            pl.BlockSpec((HALF, LANES), whole),
            pl.BlockSpec((HALF, LANES), whole),
            vec,
            vec,
            pl.BlockSpec((PANEL_TILE, FEAT), lambda i: (i, 0)),
            pl.BlockSpec((PREV, PANEL_TILE), lambda i: (0, i)),
        ],
        out_specs=(pl.BlockSpec((PANEL, PANEL_TILE), lambda i: (0, i)), pl.BlockSpec((EXT_ROWS, LANES), whole)),
        scratch_shapes=[
            pltpu.VMEM((PANEL, FEAT), BF16),
            pltpu.VMEM((2 * PANEL, PREV), BF16),
            pltpu.VMEM((PANEL, LANES), F32),
            pltpu.VMEM((PANEL, PANEL), F32),
            pltpu.VMEM((EXT, RANK), F32),
        ],
        compiler_params=pltpu.CompilerParams(vmem_limit_bytes=VMEM_LIMIT),
        cost_estimate=pl.CostEstimate(flops=2 * ROWS * RANK * 1000, bytes_accessed=ROWS * (FEAT * 2 + PREV * 4), transcendentals=0),
        name="panel",
    )(place, mine, other, diag, rhs, samples, prev_t)


def inverse8(cols):
    sub = lax.broadcasted_iota(jnp.int32, (8, LANES), 0)

    def row(x, r):
        return jnp.broadcast_to(x[r : r + 1, :], (8, LANES))

    cols = list(cols)
    for k in range(0, 8, 2):
        a, b, c = row(cols[k], k), row(cols[k + 1], k), row(cols[k + 1], k + 1)
        scale = 1.0 / (a * c - b * b)
        ia, ib, ic = c * scale, -b * scale, a * scale
        ua = cols[k] * ia + cols[k + 1] * ib
        ub = cols[k] * ib + cols[k + 1] * ic
        keep = (sub != k) & (sub != k + 1)
        first = sub == k
        for m in range(8):
            if m in (k, k + 1):
                continue
            x, y = row(cols[m], k), row(cols[m], k + 1)
            cols[m] = jnp.where(keep, cols[m] - (ua * x + ub * y), jnp.where(first, ia * x + ib * y, ib * x + ic * y))
        cols[k] = jnp.where(keep, -ua, jnp.where(first, ia, ib))
        cols[k + 1] = jnp.where(keep, -ub, jnp.where(first, ib, ic))
    return cols


def tree(terms):
    while len(terms) > 1:
        terms = [a + b for a, b in zip(terms[::2], terms[1::2])]
    return terms[0]


def inverse128(rows):
    lane = lax.broadcasted_iota(jnp.int32, (8, LANES), 1)
    sub = lax.broadcasted_iota(jnp.int32, (8, LANES), 0)
    rows = list(rows)
    n = len(rows)

    def spread(x, at):
        return jnp.broadcast_to(x[:, at : at + 1], (8, LANES))

    for p in range(n):
        inside = (lane >= 8 * p) & (lane < 8 * p + 8)
        cols = inverse8([spread(rows[p], 8 * p + j) for j in range(8)])
        own = jnp.where(inside, jnp.where(lane == sub + 8 * p, 1.0, 0.0), rows[p])
        pivot = tree([cols[j] * jnp.broadcast_to(own[j : j + 1, :], (8, LANES)) for j in range(8)])
        spread_rows = [jnp.broadcast_to(pivot[j : j + 1, :], (8, LANES)) for j in range(8)]
        rows[p] = pivot
        for step in range(1, n):
            q = (p + step) % n
            update = tree([spread(rows[q], 8 * p + j) * spread_rows[j] for j in range(8)])
            rows[q] = jnp.where(inside, 0.0, rows[q]) - update
    return rows


EXTRA = EXT - PANEL
SOLVE_AT = [sum((NB - m) * LANES + EXTRA for m in range(j)) for j in range(NB + 1)]


def solve_kernel(place_ref, mine_ref, other_ref, ext_ref, w_ref, a_ref, t_ref):
    lane = lax.broadcasted_iota(jnp.int32, (LANES, LANES), 1)
    sub = lax.broadcasted_iota(jnp.int32, (LANES, LANES), 0)

    def load(halves):
        for j in range(NB):
            for half, at, skip, n in by_half(PACKED_AT[j], PACKED_AT[j + 1]):
                to = SOLVE_AT[j] + skip
                a_ref[to : to + n, :] = halves[half][at : at + n, :]

    @pl.when(place_ref[1] == 0)
    def _():
        load((mine_ref, other_ref))

    @pl.when(place_ref[1] == 1)
    def _():
        load((other_ref, mine_ref))

    for j in range(NB):
        to = SOLVE_AT[j] + PACKED[j]
        a_ref[to : to + EXT, :] = ext_ref[EXT * j : EXT * (j + 1), :]
    to = SOLVE_AT[NB - 1]
    last = a_ref[to : to + LANES, :]
    a_ref[to : to + LANES, :] = jnp.where((lane >= PREV % LANES) & (sub < PREV % LANES), last.T, last)
    for k in range(NB):
        to = SOLVE_AT[k]
        a_ref[to : to + LANES, :] += jnp.where(lane == sub, 1.0, 0.0)
        block = inverse128([a_ref[to + 8 * i : to + 8 * i + 8, :] for i in range(LANES // 8)])
        n = (NB - k - 1) * LANES + EXTRA
        below = a_ref[to + LANES : to + LANES + n, :]
        times = mm(below, jnp.concatenate(block, axis=0), NN, HIGHEST)
        t_ref[to : to + n, :] = times
        for j in range(k + 1, NB):
            r = (j - k - 1) * LANES
            a_ref[SOLVE_AT[j] : SOLVE_AT[j] + n - r, :] -= mm(times[r:], below[r : r + LANES], NT, HIGHEST)
    weights = [None] * NB
    for k in reversed(range(NB)):
        n = (NB - k - 1) * LANES
        to = SOLVE_AT[k]
        value = t_ref[to + n : to + n + EXTRA, :]
        for i in range(k + 1, NB):
            r = to + (i - k - 1) * LANES
            value = value - mm(weights[i], t_ref[r : r + LANES, :], NN, HIGHEST)
        weights[k] = value
    for k in range(NB):
        w_ref[:, LANES * k : LANES * (k + 1)] = weights[k]


def solve(place, mine, other, ext):
    return pl.pallas_call(
        solve_kernel,
        grid=(1,),
        out_shape=jax.ShapeDtypeStruct((EXTRA, RANK), F32),
        in_specs=[
            pl.BlockSpec(memory_space=pltpu.SMEM),
            pl.BlockSpec((HALF, LANES), whole),
            pl.BlockSpec((HALF, LANES), whole),
            pl.BlockSpec((EXT_ROWS, LANES), whole),
        ],
        out_specs=pl.BlockSpec((EXTRA, RANK), whole),
        scratch_shapes=[pltpu.VMEM((SOLVE_AT[NB], LANES), F32), pltpu.VMEM((SOLVE_AT[NB], LANES), F32)],
        compiler_params=pltpu.CompilerParams(vmem_limit_bytes=VMEM_LIMIT),
        name="solve",
    )(place, mine, other, ext)


FINAL_TILE = 1024


def final_kernel(w_ref, diag_ref, rhs_ref, prev_ref, new_ref, out_ref):
    w = w_ref[...]
    wh, wl = split(jnp.concatenate([w, jnp.zeros_like(w)], axis=0))
    w = jnp.concatenate([wh, wl], axis=0)
    yh, yl = split(prev_ref[...])
    nh, nl = split(new_ref[...])
    big = mm(w[:, :PREV], yh, NN) + mm(w[:, PREV:], nh, NN)
    small = mm(wh[:, :PREV], yl, NN) + mm(wh[:, PREV:], nl, NN)
    fw = big[:1] + (big[16:17] + small[:1])
    out_ref[...] = diag_ref[...] * rhs_ref[...] - diag_ref[...] * fw


def final(w, diag, rhs, prev_t, new_t):
    vec = pl.BlockSpec((1, FINAL_TILE), lambda i: (0, i))
    return pl.pallas_call(
        final_kernel,
        grid=(ROWS // FINAL_TILE,),
        out_shape=jax.ShapeDtypeStruct((1, ROWS), F32),
        in_specs=[
            pl.BlockSpec((EXTRA, RANK), whole),
            vec,
            vec,
            pl.BlockSpec((PREV, FINAL_TILE), lambda i: (0, i)),
            pl.BlockSpec((PANEL, FINAL_TILE), lambda i: (0, i)),
        ],
        out_specs=vec,
        compiler_params=pltpu.CompilerParams(vmem_limit_bytes=VMEM_LIMIT),
        name="final",
    )(w, diag, rhs, prev_t, new_t)


SAME_CORE = [[i for i in range(128) if i % 2 == core] for core in range(2)]
OTHER_CORE = [(i, i ^ 1) for i in range(128)]


def sum_large(keep, send):
    shape = keep.shape
    keep = (keep + lax.ppermute(send, AXES, OTHER_CORE)).reshape(64, -1, LANES)
    parts = lax.all_to_all(keep, AXES, 0, 0, axis_index_groups=SAME_CORE)
    part = jnp.sum(parts, axis=0)
    mine = lax.all_to_all(jnp.broadcast_to(part, parts.shape), AXES, 0, 0, axis_index_groups=SAME_CORE)
    mine = mine.reshape(shape)
    return mine, lax.ppermute(mine, AXES, OTHER_CORE)


def sum_small(x):
    parts = lax.all_to_all(x.reshape(128, -1, LANES), AXES, 0, 0)
    part = jnp.sum(parts, axis=0)
    return lax.all_to_all(jnp.broadcast_to(part, parts.shape), AXES, 0, 0).reshape(x.shape)


def on_device(samples, prev_factor, pivots, inv_diag, rhs):
    index = lax.axis_index(AXES)
    place = jnp.stack([index * ROWS, index % 2]).astype(jnp.int32)
    diag, rhs = inv_diag.reshape(1, ROWS), rhs.reshape(1, ROWS)
    prev_t = prev_factor.T
    keep, send = gram(samples, prev_t, pivots, diag, place)
    mine, other = sum_large(keep, send)
    new_t, ext = panel(place, mine, other, diag, rhs, samples, prev_t)
    ext = sum_small(ext)
    w = solve(place, mine, other, ext)
    out = final(w, diag, rhs, prev_t, new_t)
    return (new_t.T, out.reshape(ROWS))


def solution(mesh):
    return jax.shard_map(
        on_device,
        mesh=mesh,
        in_specs=(
            P(AXES, None),
            P(AXES, None),
            P(),
            P(AXES),
            P(AXES),
        ),
        out_specs=(P(AXES, None), P(AXES)),
        check_vma=False,
    )
```

```python
import functools

import jax
import jax.numpy as jnp
from jax import lax
from jax.experimental import pallas as pl
from jax.experimental.pallas import tpu as pltpu
from jax.sharding import PartitionSpec as P

FEAT = 2048
PREV = 992
PANEL = 32
RANK = 1024
ROWS = 2048
LANES = 128
NB = RANK // LANES
PACKED = [PREV - j * LANES for j in range(NB)]
PACKED_AT = [sum(PACKED[:j]) for j in range(NB + 1)]
GRAM_ROWS = PACKED_AT[NB]
PICK_ROWS = PANEL * (FEAT + RANK) // LANES
SEND_ROWS = GRAM_ROWS + PICK_ROWS
HALF = SEND_ROWS // 2
EXT = 40
EXT_ROWS = 512
HIGHEST = lax.Precision.HIGHEST
F32 = jnp.float32
BF16 = jnp.bfloat16
AXES = ("row", "col")
VMEM_LIMIT = 50 * 2**20


def split(x):
    high = x.astype(BF16)
    return high, (x - high.astype(F32)).astype(BF16)


def mm(a, b, dims, precision=None):
    return lax.dot_general(a, b, (dims, ((), ())), precision=precision, preferred_element_type=F32)


NN = ((1,), (0,))
NT = ((1,), (1,))


def column(row):
    return jnp.broadcast_to(row, (LANES, LANES)).T


def whole(i):
    return (0, 0)


def by_half(start, stop):
    cuts = [start] + [HALF] * (start < HALF < stop) + [stop]
    return [(a // HALF, a % HALF, a - start, b - a) for a, b in zip(cuts, cuts[1:])]


GRAM_TILE = 512


def gram_kernel(pivots_ref, place_ref, diag_ref, samples_ref, prev_ref, keep_ref, send_ref, acc_ref, picks_ref, srow_ref, sem):
    step = pl.program_id(0)
    base = place_ref[0]

    def row_copy(p):
        start = pl.multiple_of((pivots_ref[p] - base) // 16 * 16, 16)
        return pltpu.make_async_copy(samples_ref.at[pl.ds(start, 16)], srow_ref.at[p], sem.at[p])

    def owned(p):
        place = pivots_ref[p] - base
        return (place >= 0) & (place < ROWS)

    @pl.when(step == 0)
    def _():
        acc_ref[...] = jnp.zeros_like(acc_ref)
        picks_ref[...] = jnp.zeros_like(picks_ref)

        def start(p, carry):
            @pl.when(owned(p))
            def _():
                row_copy(p).start()

            return carry

        lax.fori_loop(0, PANEL, start, 0)

    high, low = split(prev_ref[...] * jnp.sqrt(diag_ref[...]))
    at = 0
    for j in range(4):
        first = 256 * j
        wide = min(256, PREV - first)
        mine_h, mine_l = high[first : first + wide], low[first : first + wide]
        total = mm(high[first:], mine_h, NT) + (mm(high[first:], mine_l, NT) + mm(low[first:], mine_h, NT))
        acc_ref[at : at + PREV - first, :wide] += total
        at += PREV - first

    def factor_row(p, carry):
        place = pivots_ref[p] - base

        @pl.when(owned(p) & (place // GRAM_TILE == step))
        def _():
            local = place % GRAM_TILE
            start = pl.multiple_of(local // LANES * LANES, LANES)
            chosen = lax.broadcasted_iota(jnp.int32, (8, LANES), 1) == local % LANES
            row = mm(jnp.where(chosen, 1.0, 0.0), prev_ref[:, pl.ds(start, LANES)], NT, HIGHEST)[:1]
            to = PANEL * FEAT // LANES
            for c in range(NB - 1):
                picks_ref[pl.ds(to + c * PANEL + p, 1), :] = row[:, c * LANES : (c + 1) * LANES]
            picks_ref[pl.ds(to + (NB - 1) * PANEL + p, 1), : PREV % LANES] = row[:, (NB - 1) * LANES :]

        return carry

    lax.fori_loop(0, PANEL, factor_row, 0)

    @pl.when(step == ROWS // GRAM_TILE - 1)
    def _():
        def sample_row(p, carry):
            @pl.when(owned(p))
            def _():
                row_copy(p).wait()
                sub = lax.broadcasted_iota(jnp.int32, (16, FEAT), 0)
                row = jnp.sum(jnp.where(sub == (pivots_ref[p] - base) % 16, srow_ref[p].astype(F32), 0.0), axis=0, keepdims=True)
                for c in range(FEAT // LANES):
                    picks_ref[pl.ds(c * PANEL + p, 1), :] = row[:, c * LANES : (c + 1) * LANES]

            return carry

        lax.fori_loop(0, PANEL, sample_row, 0)

        def write(halves):
            at = 0
            for j in range(NB):
                lane = (j % 2) * LANES
                wide = min(LANES, PREV - j * LANES)
                for half, to, skip, n in by_half(PACKED_AT[j], PACKED_AT[j + 1]):
                    halves[half][to : to + n, :wide] = acc_ref[at + lane + skip : at + lane + skip + n, lane : lane + wide]
                    if wide < LANES:
                        halves[half][to : to + n, wide:] = jnp.zeros((n, LANES - wide), F32)
                at += (PREV - j * LANES + LANES) * (j % 2)
            halves[1][GRAM_ROWS - HALF :, :] = picks_ref[...]

        @pl.when(place_ref[1] == 0)
        def _():
            write((keep_ref, send_ref))

        @pl.when(place_ref[1] == 1)
        def _():
            write((send_ref, keep_ref))


def gram(samples, prev_t, pivots, diag, place):
    half = jax.ShapeDtypeStruct((HALF, LANES), F32)
    return pl.pallas_call(
        gram_kernel,
        grid=(ROWS // GRAM_TILE,),
        out_shape=(half, half),
        in_specs=[
            pl.BlockSpec(memory_space=pltpu.SMEM),
            pl.BlockSpec(memory_space=pltpu.SMEM),
            pl.BlockSpec((1, GRAM_TILE), lambda i: (0, i)),
            pl.BlockSpec(memory_space=pl.ANY),
            pl.BlockSpec((PREV, GRAM_TILE), lambda i: (0, i)),
        ],
        out_specs=(pl.BlockSpec((HALF, LANES), whole), pl.BlockSpec((HALF, LANES), whole)),
        scratch_shapes=[
            pltpu.VMEM((sum(PREV - 256 * j for j in range(4)), 256), F32),
            pltpu.VMEM((PICK_ROWS, LANES), F32),
            pltpu.VMEM((PANEL, 16, FEAT), BF16),
            pltpu.SemaphoreType.DMA((PANEL,)),
        ],
        compiler_params=pltpu.CompilerParams(vmem_limit_bytes=VMEM_LIMIT),
        cost_estimate=pl.CostEstimate(flops=6 * ROWS * RANK * 640, bytes_accessed=ROWS * PREV * 4, transcendentals=0),
        name="gram",
    )(pivots, place, diag, samples, prev_t)


PANEL_TILE = 512


def panel_kernel(place_ref, mine_ref, other_ref, diag_ref, rhs_ref, samples_ref, prev_ref, new_ref, ext_ref, picked_ref, pfac_ref, norm_ref, inv_ref, acc_ref):
    step = pl.program_id(0)
    nfeat = FEAT // LANES

    def prepare(picks_ref):
        def pick(c):
            return picks_ref[GRAM_ROWS - HALF + c * PANEL : GRAM_ROWS - HALF + (c + 1) * PANEL, :]

        acc_ref[...] = jnp.zeros_like(acc_ref)
        picked = jnp.concatenate([pick(c) for c in range(nfeat)], axis=1)
        pfac = jnp.concatenate([pick(nfeat + c) for c in range(NB)], axis=1)[:, :PREV]
        picked16 = picked.astype(BF16)
        picked_ref[...] = picked16
        high, low = split(pfac)
        pfac_ref[:PANEL, :] = high
        pfac_ref[PANEL:, :] = low
        square = picked * picked
        norm_row = mm(jnp.ones((8, FEAT), F32), square, NT, HIGHEST)[:1]
        norm_col = jnp.sum(square, axis=1, keepdims=True)
        norm_ref[...] = jnp.broadcast_to(norm_col, (PANEL, LANES))
        cross = mm(picked16, picked16, NT)
        dist = jnp.maximum(norm_col + norm_row - 2.0 * cross, 0.0)
        a = jnp.exp(-(2.0 / FEAT) * dist) - mm(pfac, pfac, NT, HIGHEST)
        sub = lax.broadcasted_iota(jnp.int32, (PANEL, PANEL), 0)
        lane = lax.broadcasted_iota(jnp.int32, (PANEL, PANEL), 1)
        b = jnp.where(sub == lane, 1.0, 0.0)
        for k in range(PANEL - 1):
            factor = jnp.where(sub > k, a[:, k : k + 1] / a[k : k + 1, k : k + 1], 0.0)
            a, b = a - factor * a[k : k + 1, :], b - factor * b[k : k + 1, :]
        pivot = jnp.sum(jnp.where(sub == lane, a, 0.0), axis=1, keepdims=True)
        inv_ref[...] = b / jnp.sqrt(pivot)

    @pl.when((step == 0) & (place_ref[1] == 1))
    def _():
        prepare(mine_ref)

    @pl.when((step == 0) & (place_ref[1] == 0))
    def _():
        prepare(other_ref)

    tile = samples_ref[...]
    squares = None
    for c in range(nfeat):
        part = tile[:, c * LANES : (c + 1) * LANES].astype(F32)
        squares = part * part if squares is None else squares + part * part
    norm = jnp.concatenate(
        [jnp.sum(squares[c : c + LANES].T, axis=0, keepdims=True) for c in range(0, PANEL_TILE, LANES)], axis=1
    )
    cross = mm(picked_ref[...], tile, NT)
    dist = jnp.maximum(norm + norm_ref[:, :1] - 2.0 * cross, 0.0)
    high, low = split(prev_ref[...])
    both = mm(pfac_ref[...], high, NN)
    inner = both[:PANEL] + (both[PANEL:] + mm(pfac_ref[:PANEL, :], low, NN))
    resid = jnp.exp(-(2.0 / FEAT) * dist) - inner
    new = mm(inv_ref[...], resid, NN, HIGHEST)
    new_ref[...] = new
    sub = lax.broadcasted_iota(jnp.int32, (EXT - PANEL, PANEL_TILE), 0)
    x = diag_ref[...] * jnp.concatenate([new, jnp.where(sub == 0, rhs_ref[...], 0.0)], axis=0)
    x = jnp.concatenate([x, jnp.zeros((48 - EXT, PANEL_TILE), F32)], axis=0)
    xh, xl = split(x)
    nh, nl = split(new)
    high, low = jnp.concatenate([high, nh], axis=0), jnp.concatenate([low, nl], axis=0)
    both = mm(jnp.concatenate([xh, xl], axis=0), high, NT)
    acc_ref[...] += both[:EXT] + (both[48 : 48 + EXT] + mm(xh, low, NT)[:EXT])

    @pl.when(step == ROWS // PANEL_TILE - 1)
    def _():
        for c in range(NB):
            ext_ref[EXT * c : EXT * (c + 1), :] = acc_ref[:, c * LANES : (c + 1) * LANES]
        ext_ref[EXT * NB :, :] = jnp.zeros((EXT_ROWS - EXT * NB, LANES), F32)


def panel(place, mine, other, diag, rhs, samples, prev_t):
    vec = pl.BlockSpec((1, PANEL_TILE), lambda i: (0, i))
    return pl.pallas_call(
        panel_kernel,
        grid=(ROWS // PANEL_TILE,),
        out_shape=(jax.ShapeDtypeStruct((PANEL, ROWS), F32), jax.ShapeDtypeStruct((EXT_ROWS, LANES), F32)),
        in_specs=[
            pl.BlockSpec(memory_space=pltpu.SMEM),
            pl.BlockSpec((HALF, LANES), whole),
            pl.BlockSpec((HALF, LANES), whole),
            vec,
            vec,
            pl.BlockSpec((PANEL_TILE, FEAT), lambda i: (i, 0)),
            pl.BlockSpec((PREV, PANEL_TILE), lambda i: (0, i)),
        ],
        out_specs=(pl.BlockSpec((PANEL, PANEL_TILE), lambda i: (0, i)), pl.BlockSpec((EXT_ROWS, LANES), whole)),
        scratch_shapes=[
            pltpu.VMEM((PANEL, FEAT), BF16),
            pltpu.VMEM((2 * PANEL, PREV), BF16),
            pltpu.VMEM((PANEL, LANES), F32),
            pltpu.VMEM((PANEL, PANEL), F32),
            pltpu.VMEM((EXT, RANK), F32),
        ],
        compiler_params=pltpu.CompilerParams(vmem_limit_bytes=VMEM_LIMIT),
        cost_estimate=pl.CostEstimate(flops=2 * ROWS * RANK * 1000, bytes_accessed=ROWS * (FEAT * 2 + PREV * 4), transcendentals=0),
        name="panel",
    )(place, mine, other, diag, rhs, samples, prev_t)


def inverse8(cols):
    sub = lax.broadcasted_iota(jnp.int32, (8, LANES), 0)

    def row(x, r):
        return jnp.broadcast_to(x[r : r + 1, :], (8, LANES))

    cols = list(cols)
    for k in range(0, 8, 2):
        a, b, c = row(cols[k], k), row(cols[k + 1], k), row(cols[k + 1], k + 1)
        scale = 1.0 / (a * c - b * b)
        ia, ib, ic = c * scale, -b * scale, a * scale
        ua = cols[k] * ia + cols[k + 1] * ib
        ub = cols[k] * ib + cols[k + 1] * ic
        keep = (sub != k) & (sub != k + 1)
        first = sub == k
        for m in range(8):
            if m in (k, k + 1):
                continue
            x, y = row(cols[m], k), row(cols[m], k + 1)
            cols[m] = jnp.where(keep, cols[m] - (ua * x + ub * y), jnp.where(first, ia * x + ib * y, ib * x + ic * y))
        cols[k] = jnp.where(keep, -ua, jnp.where(first, ia, ib))
        cols[k + 1] = jnp.where(keep, -ub, jnp.where(first, ib, ic))
    return cols


def tree(terms):
    while len(terms) > 1:
        terms = [a + b for a, b in zip(terms[::2], terms[1::2])]
    return terms[0]


def inverse128(rows):
    lane = lax.broadcasted_iota(jnp.int32, (8, LANES), 1)
    sub = lax.broadcasted_iota(jnp.int32, (8, LANES), 0)
    rows = list(rows)
    n = len(rows)

    def spread(x, at):
        return jnp.broadcast_to(x[:, at : at + 1], (8, LANES))

    for p in range(n):
        inside = (lane >= 8 * p) & (lane < 8 * p + 8)
        cols = inverse8([spread(rows[p], 8 * p + j) for j in range(8)])
        own = jnp.where(inside, jnp.where(lane == sub + 8 * p, 1.0, 0.0), rows[p])
        pivot = tree([cols[j] * jnp.broadcast_to(own[j : j + 1, :], (8, LANES)) for j in range(8)])
        spread_rows = [jnp.broadcast_to(pivot[j : j + 1, :], (8, LANES)) for j in range(8)]
        rows[p] = pivot
        for step in range(1, n):
            q = (p + step) % n
            update = tree([spread(rows[q], 8 * p + j) * spread_rows[j] for j in range(8)])
            rows[q] = jnp.where(inside, 0.0, rows[q]) - update
        yield
    return rows


EXTRA = EXT - PANEL


def three(x):
    high = x.astype(BF16)
    rest = x - high.astype(F32)
    mid = rest.astype(BF16)
    return high, mid, (rest - mid.astype(F32)).astype(BF16)


def left_parts(x):
    h, m, lo = three(x)
    return jnp.concatenate([h, m], axis=1), jnp.concatenate([h, lo], axis=1)


def right_parts(x, axis):
    h, m, lo = three(x)
    return tuple(jnp.concatenate(pair, axis=axis) for pair in ((h, h), (m, m), (lo, h)))


def product(left, right, dims):
    return mm(left[0], right[0], dims) + (mm(left[0], right[1], dims) + mm(left[1], right[2], dims))


def run(steps, fillers):
    count = LANES // 8
    done = 0
    for i in range(count + 1):
        try:
            next(steps)
        except StopIteration as end:
            for filler in fillers[done:]:
                filler()
            return end.value
        upto = len(fillers) * (i + 1) // count
        for filler in fillers[done:upto]:
            filler()
        done = upto


def eliminate(first, last, cols, t_refs, inv_ref):
    fillers = []
    for k in range(first, last):
        ref, at = cols[k]
        n = PACKED[k] - LANES
        block = run(inverse128([ref[at + 8 * i : at + 8 * i + 8, :] for i in range(LANES // 8)]), fillers)
        block = jnp.concatenate(block, axis=0)
        inv_ref[(k - first) * LANES : (k - first + 1) * LANES, :] = block
        weights = right_parts(block, 0)
        below = ref[at + LANES : at + LANES + n, :]
        left = left_parts(below)
        right = right_parts(below, 1)
        times = product(left, weights, NN)
        t_refs[k][...] = times
        times = left_parts(times)

        def update(j, lo, hi, wide, times=times, right=right, k=k):
            r = (j - k - 1) * LANES
            value = product(tuple(x[lo:hi] for x in times), tuple(x[r : r + wide] for x in right), NT)
            for c in range(0, wide, LANES):
                to_ref, to = cols[j + c // LANES]
                start = max(lo, r + c)
                to += start - (r + c)
                w = min(LANES, wide - c)
                to_ref[to : to + hi - start, :w] -= value[start - lo :, c : c + w]

        update(k + 1, 0, min(LANES, n), min(LANES, n))
        fillers = []
        if n > LANES:
            fillers.append(functools.partial(update, k + 1, LANES, n, LANES))
        for j in range(k + 2, NB, 2):
            r = (j - k - 1) * LANES
            fillers.append(functools.partial(update, j, r, n, min(2 * LANES, n - r)))
    for filler in fillers:
        filler()


CUTS = (0, 4, 7)
LEFT = [PACKED_AT[j] - PACKED_AT[CUTS[1]] for j in range(CUTS[1], NB + 1)]


def solve_first_kernel(place_ref, mine_ref, other_ref, left_ref, inv_ref, *refs):
    t_refs, a_ref = refs[:-1], refs[-1]
    lane = lax.broadcasted_iota(jnp.int32, (LANES, LANES), 1)
    sub = lax.broadcasted_iota(jnp.int32, (LANES, LANES), 0)

    def load(halves):
        for half, at, to, n in by_half(0, PACKED_AT[CUTS[1]]):
            a_ref[to : to + n, :] = halves[half][at : at + n, :]
        for half, at, to, n in by_half(PACKED_AT[CUTS[1]], GRAM_ROWS):
            left_ref[to : to + n, :] = halves[half][at : at + n, :]

    @pl.when(place_ref[1] == 0)
    def _():
        load((mine_ref, other_ref))

    @pl.when(place_ref[1] == 1)
    def _():
        load((other_ref, mine_ref))

    cols = [(a_ref, PACKED_AT[j]) for j in range(CUTS[1])] + [(left_ref, LEFT[j - CUTS[1]]) for j in range(CUTS[1], NB)]
    for j, (ref, at) in enumerate(cols):
        n = min(LANES, PACKED[j])
        ref[at : at + n, :] += jnp.where(lane == sub, 1.0, 0.0)[:n]
    eliminate(0, CUTS[1], cols, dict(enumerate(t_refs)), inv_ref)


def solve_second_kernel(left_ref, last_ref, inv_ref, *refs):
    t_refs, a_ref = refs[:-1], refs[-1]
    a_ref[...] = left_ref[...]
    eliminate(CUTS[1], CUTS[2], {j: (a_ref, LEFT[j - CUTS[1]]) for j in range(CUTS[1], NB)}, {CUTS[1] + i: r for i, r in enumerate(t_refs)}, inv_ref)
    last_ref[...] = a_ref[LEFT[-2] :, :]


def solve_last_kernel(last_ref, inv0_ref, inv1_ref, ext_ref, *refs):
    t_refs, w_ref, e_ref = refs[: NB - 1], refs[NB - 1], refs[NB]
    tail = PREV % LANES
    for j in range(NB):
        e_ref[:, j * LANES : (j + 1) * LANES] = ext_ref[EXT * j : EXT * (j + 1), :]
    scaled = []
    for k in range(NB - 1):
        here = e_ref[:, k * LANES : (k + 1) * LANES]
        left = left_parts(here)
        n = PACKED[k] - LANES
        change = product(left, right_parts(t_refs[k][...], 1), NT)
        e_ref[:, (k + 1) * LANES : PREV] -= change
        inv = inv0_ref[k * LANES : (k + 1) * LANES, :] if k < CUTS[1] else inv1_ref[(k - CUTS[1]) * LANES : (k - CUTS[1] + 1) * LANES, :]
        times = product(left, right_parts(inv, 0), NN)
        scaled.append(times)
        corner = product(left, right_parts(times, 1), NT)
        total = corner if k == 0 else total + corner
    lane = lax.broadcasted_iota(jnp.int32, (LANES, LANES), 1)
    sub = lax.broadcasted_iota(jnp.int32, (LANES, LANES), 0)
    shifted = jnp.concatenate([jnp.zeros((EXT, tail), F32), total[:, :PANEL]], axis=1)
    bottom = e_ref[:, (NB - 1) * LANES :] - shifted
    bottom = bottom + jnp.where(lax.broadcasted_iota(jnp.int32, (EXT, LANES), 1) == lax.broadcasted_iota(jnp.int32, (EXT, LANES), 0) + tail, 1.0, 0.0)
    block = jnp.concatenate([last_ref[...], bottom[:PANEL]], axis=0)
    block = jnp.where((lane >= tail) & (sub < tail), block.T, block)
    inverse = run(inverse128([block[8 * i : 8 * i + 8, :] for i in range(LANES // 8)]), [])
    inverse = jnp.concatenate(inverse, axis=0)
    value = mm(bottom[PANEL:], inverse, NN, HIGHEST)
    w_ref[:, (NB - 1) * LANES :] = value
    sums = [None] * (NB - 1)
    for k in reversed(range(1, NB)):
        spread = column(value[:1])
        for j in range(k):
            r = (k - j - 1) * LANES
            rows = t_refs[j][r : r + min(LANES, PREV - k * LANES), :]
            if k == NB - 1:
                rows = jnp.concatenate([rows, scaled[j][:PANEL]], axis=0)
            part = (rows * spread).reshape(LANES // 8, 8, LANES).sum(axis=0)
            sums[j] = part if sums[j] is None else sums[j] + part
        value = scaled[k - 1][PANEL:] - jnp.sum(sums[k - 1], axis=0, keepdims=True)
        w_ref[:, (k - 1) * LANES : k * LANES] = value


def block_spec(rows):
    return pl.BlockSpec((rows, LANES), whole)


def shape(rows):
    return jax.ShapeDtypeStruct((rows, LANES), F32)


def solve_first(place, mine, other):
    below = [PACKED[k] - LANES for k in range(CUTS[1])]
    outs = [LEFT[-1], CUTS[1] * LANES] + below
    return pl.pallas_call(
        solve_first_kernel,
        grid=(1,),
        out_shape=tuple(shape(r) for r in outs),
        in_specs=[pl.BlockSpec(memory_space=pltpu.SMEM), block_spec(HALF), block_spec(HALF)],
        out_specs=tuple(block_spec(r) for r in outs),
        scratch_shapes=[pltpu.VMEM((PACKED_AT[CUTS[1]], LANES), F32)],
        compiler_params=pltpu.CompilerParams(vmem_limit_bytes=VMEM_LIMIT),
        cost_estimate=pl.CostEstimate(flops=2 * 10**10, bytes_accessed=10**7, transcendentals=0),
        name="solve_first",
    )(place, mine, other)


def solve_second(left):
    below = [PACKED[k] - LANES for k in range(CUTS[1], CUTS[2])]
    outs = [PACKED[NB - 1], (CUTS[2] - CUTS[1]) * LANES] + below
    return pl.pallas_call(
        solve_second_kernel,
        grid=(1,),
        out_shape=tuple(shape(r) for r in outs),
        in_specs=[block_spec(LEFT[-1])],
        out_specs=tuple(block_spec(r) for r in outs),
        scratch_shapes=[pltpu.VMEM((LEFT[-1], LANES), F32)],
        compiler_params=pltpu.CompilerParams(vmem_limit_bytes=VMEM_LIMIT),
        cost_estimate=pl.CostEstimate(flops=2 * 10**10, bytes_accessed=10**7, transcendentals=0),
        name="solve_second",
    )(left)


def solve_last(last, inv0, inv1, ext, t):
    ins = [PACKED[NB - 1], CUTS[1] * LANES, (CUTS[2] - CUTS[1]) * LANES, EXT_ROWS] + [PACKED[k] - LANES for k in range(NB - 1)]
    return pl.pallas_call(
        solve_last_kernel,
        grid=(1,),
        out_shape=jax.ShapeDtypeStruct((EXTRA, RANK), F32),
        in_specs=[block_spec(r) for r in ins],
        out_specs=pl.BlockSpec((EXTRA, RANK), whole),
        scratch_shapes=[pltpu.VMEM((EXT, RANK), F32)],
        compiler_params=pltpu.CompilerParams(vmem_limit_bytes=VMEM_LIMIT),
        name="solve_last",
    )(last, inv0, inv1, ext, *t)


FINAL_TILE = 1024


def final_kernel(w_ref, diag_ref, rhs_ref, prev_ref, new_ref, out_ref):
    w = w_ref[...]
    wh, wl = split(jnp.concatenate([w, jnp.zeros_like(w)], axis=0))
    w = jnp.concatenate([wh, wl], axis=0)
    yh, yl = split(prev_ref[...])
    nh, nl = split(new_ref[...])
    big = mm(w[:, :PREV], yh, NN) + mm(w[:, PREV:], nh, NN)
    small = mm(wh[:, :PREV], yl, NN) + mm(wh[:, PREV:], nl, NN)
    fw = big[:1] + (big[16:17] + small[:1])
    out_ref[...] = diag_ref[...] * rhs_ref[...] - diag_ref[...] * fw


def final(w, diag, rhs, prev_t, new_t):
    vec = pl.BlockSpec((1, FINAL_TILE), lambda i: (0, i))
    return pl.pallas_call(
        final_kernel,
        grid=(ROWS // FINAL_TILE,),
        out_shape=jax.ShapeDtypeStruct((1, ROWS), F32),
        in_specs=[
            pl.BlockSpec((EXTRA, RANK), whole),
            vec,
            vec,
            pl.BlockSpec((PREV, FINAL_TILE), lambda i: (0, i)),
            pl.BlockSpec((PANEL, FINAL_TILE), lambda i: (0, i)),
        ],
        out_specs=vec,
        compiler_params=pltpu.CompilerParams(vmem_limit_bytes=VMEM_LIMIT),
        name="final",
    )(w, diag, rhs, prev_t, new_t)


SAME_CORE = [[i for i in range(128) if i % 2 == core] for core in range(2)]
OTHER_CORE = [(i, i ^ 1) for i in range(128)]


def sum_large(keep, send):
    shape = keep.shape
    keep = (keep + lax.ppermute(send, AXES, OTHER_CORE)).reshape(64, -1, LANES)
    parts = lax.all_to_all(keep, AXES, 0, 0, axis_index_groups=SAME_CORE)
    part = jnp.sum(parts, axis=0)
    mine = lax.all_to_all(jnp.broadcast_to(part, parts.shape), AXES, 0, 0, axis_index_groups=SAME_CORE)
    mine = mine.reshape(shape)
    return mine, lax.ppermute(mine, AXES, OTHER_CORE)


def on_device(samples, prev_factor, pivots, inv_diag, rhs):
    index = lax.axis_index(AXES)
    place = jnp.stack([index * ROWS, index % 2]).astype(jnp.int32)
    diag, rhs = inv_diag.reshape(1, ROWS), rhs.reshape(1, ROWS)
    prev_t = prev_factor.T
    keep, send = gram(samples, prev_t, pivots, diag, place)
    mine, other = sum_large(keep, send)
    new_t, ext = panel(place, mine, other, diag, rhs, samples, prev_t)
    parts = lax.all_to_all(ext.reshape(128, -1, LANES), AXES, 0, 0)
    left, inv0, *t0 = solve_first(place, mine, other)
    parts, left = lax.optimization_barrier((parts, left))
    part = jnp.sum(parts, axis=0)
    ext = lax.all_to_all(jnp.broadcast_to(part, parts.shape), AXES, 0, 0).reshape(ext.shape)
    last, inv1, *t1 = solve_second(left)
    w = solve_last(last, inv0, inv1, ext, t0 + t1)
    out = final(w, diag, rhs, prev_t, new_t)
    return (new_t.T, out.reshape(ROWS))


def solution(mesh):
    return jax.shard_map(
        on_device,
        mesh=mesh,
        in_specs=(
            P(AXES, None),
            P(AXES, None),
            P(),
            P(AXES),
            P(AXES),
        ),
        out_specs=(P(AXES, None), P(AXES)),
        check_vma=False,
    )
```

```python
import functools

import jax
import jax.numpy as jnp
from jax import lax
from jax.experimental import pallas as pl
from jax.experimental.pallas import tpu as pltpu
from jax.sharding import PartitionSpec as P

FEAT = 2048
PREV = 992
PANEL = 32
RANK = 1024
ROWS = 2048
LANES = 128
NB = RANK // LANES
PACKED = [PREV - j * LANES for j in range(NB)]
PACKED_AT = [sum(PACKED[:j]) for j in range(NB + 1)]
GRAM_ROWS = PACKED_AT[NB]
PICK_ROWS = PANEL * (FEAT + RANK) // LANES
SEND_ROWS = GRAM_ROWS + PICK_ROWS
HALF = SEND_ROWS // 2
EXT = 40
EXT_ROWS = 512
HIGHEST = lax.Precision.HIGHEST
F32 = jnp.float32
BF16 = jnp.bfloat16
AXES = ("row", "col")
VMEM_LIMIT = 50 * 2**20


def split(x):
    high = x.astype(BF16)
    return high, (x - high.astype(F32)).astype(BF16)


def three(x):
    high = x.astype(BF16)
    rest = x - high.astype(F32)
    mid = rest.astype(BF16)
    return high, mid, (rest - mid.astype(F32)).astype(BF16)


def mm(a, b, dims, precision=None):
    return lax.dot_general(a, b, (dims, ((), ())), precision=precision, preferred_element_type=F32)


NN = ((1,), (0,))
NT = ((1,), (1,))


def column(row):
    return jnp.broadcast_to(row, (LANES, LANES)).T


def whole(i):
    return (0, 0)


def by_half(start, stop):
    cuts = [start] + [HALF] * (start < HALF < stop) + [stop]
    return [(a // HALF, a % HALF, a - start, b - a) for a, b in zip(cuts, cuts[1:])]


GRAM_TILE = 1024


def gram_kernel(pivots_ref, place_ref, diag_ref, samples_ref, prev_ref, keep_ref, send_ref, acc_ref, picks_ref, srow_ref, sem):
    step = pl.program_id(0)
    base = place_ref[0]

    def row_copy(p):
        start = pl.multiple_of((pivots_ref[p] - base) // 16 * 16, 16)
        return pltpu.make_async_copy(samples_ref.at[pl.ds(start, 16)], srow_ref.at[p], sem.at[p])

    def owned(p):
        place = pivots_ref[p] - base
        return (place >= 0) & (place < ROWS)

    @pl.when(step == 0)
    def _():
        acc_ref[...] = jnp.zeros_like(acc_ref)
        picks_ref[...] = jnp.zeros_like(picks_ref)

        def start(p, carry):
            @pl.when(owned(p))
            def _():
                row_copy(p).start()

            return carry

        lax.fori_loop(0, PANEL, start, 0)

    high, low = split(prev_ref[...] * jnp.sqrt(diag_ref[...]))
    at = 0
    for j in range(4):
        first = 256 * j
        wide = min(256, PREV - first)
        mine_h, mine_l = high[first : first + wide], low[first : first + wide]
        total = mm(high[first:], mine_h, NT) + (mm(high[first:], mine_l, NT) + mm(low[first:], mine_h, NT))
        acc_ref[at : at + PREV - first, :wide] += total
        at += PREV - first

    def factor_row(p, carry):
        place = pivots_ref[p] - base

        @pl.when(owned(p) & (place // GRAM_TILE == step))
        def _():
            local = place % GRAM_TILE
            start = pl.multiple_of(local // LANES * LANES, LANES)
            chosen = lax.broadcasted_iota(jnp.int32, (16, LANES), 1) == local % LANES
            chosen = jnp.where(chosen, 1.0, 0.0).astype(BF16)
            parts = three(prev_ref[:, pl.ds(start, LANES)])
            row = (mm(chosen, parts[0], NT) + mm(chosen, parts[1], NT) + mm(chosen, parts[2], NT))[:1]
            to = PANEL * FEAT // LANES
            for c in range(NB - 1):
                picks_ref[pl.ds(to + c * PANEL + p, 1), :] = row[:, c * LANES : (c + 1) * LANES]
            picks_ref[pl.ds(to + (NB - 1) * PANEL + p, 1), : PREV % LANES] = row[:, (NB - 1) * LANES :]

        return carry

    lax.fori_loop(0, PANEL, factor_row, 0)

    @pl.when(step == ROWS // GRAM_TILE - 1)
    def _():
        def sample_row(p, carry):
            @pl.when(owned(p))
            def _():
                row_copy(p).wait()
                sub = lax.broadcasted_iota(jnp.int32, (16, FEAT), 0)
                row = jnp.sum(jnp.where(sub == (pivots_ref[p] - base) % 16, srow_ref[p].astype(F32), 0.0), axis=0, keepdims=True)
                for c in range(FEAT // LANES):
                    picks_ref[pl.ds(c * PANEL + p, 1), :] = row[:, c * LANES : (c + 1) * LANES]

            return carry

        lax.fori_loop(0, PANEL, sample_row, 0)

        def write(halves):
            at = 0
            for j in range(NB):
                lane = (j % 2) * LANES
                wide = min(LANES, PREV - j * LANES)
                for half, to, skip, n in by_half(PACKED_AT[j], PACKED_AT[j + 1]):
                    halves[half][to : to + n, :wide] = acc_ref[at + lane + skip : at + lane + skip + n, lane : lane + wide]
                    if wide < LANES:
                        halves[half][to : to + n, wide:] = jnp.zeros((n, LANES - wide), F32)
                at += (PREV - j * LANES + LANES) * (j % 2)
            halves[1][GRAM_ROWS - HALF :, :] = picks_ref[...]

        @pl.when(place_ref[1] == 0)
        def _():
            write((keep_ref, send_ref))

        @pl.when(place_ref[1] == 1)
        def _():
            write((send_ref, keep_ref))


def gram(samples, prev_t, pivots, diag, place):
    half = jax.ShapeDtypeStruct((HALF, LANES), F32)
    return pl.pallas_call(
        gram_kernel,
        grid=(ROWS // GRAM_TILE,),
        out_shape=(half, half),
        in_specs=[
            pl.BlockSpec(memory_space=pltpu.SMEM),
            pl.BlockSpec(memory_space=pltpu.SMEM),
            pl.BlockSpec((1, GRAM_TILE), lambda i: (0, i)),
            pl.BlockSpec(memory_space=pl.ANY),
            pl.BlockSpec((PREV, GRAM_TILE), lambda i: (0, i)),
        ],
        out_specs=(pl.BlockSpec((HALF, LANES), whole), pl.BlockSpec((HALF, LANES), whole)),
        scratch_shapes=[
            pltpu.VMEM((sum(PREV - 256 * j for j in range(4)), 256), F32),
            pltpu.VMEM((PICK_ROWS, LANES), F32),
            pltpu.VMEM((PANEL, 16, FEAT), BF16),
            pltpu.SemaphoreType.DMA((PANEL,)),
        ],
        compiler_params=pltpu.CompilerParams(vmem_limit_bytes=VMEM_LIMIT),
        cost_estimate=pl.CostEstimate(flops=6 * ROWS * RANK * 640, bytes_accessed=ROWS * PREV * 4, transcendentals=0),
        name="gram",
    )(pivots, place, diag, samples, prev_t)


PANEL_TILE = 512


def panel_kernel(place_ref, mine_ref, other_ref, diag_ref, rhs_ref, samples_ref, prev_ref, new_ref, ext_ref, picked_ref, pfac_ref, norm_ref, inv_ref, acc_ref):
    step = pl.program_id(0)
    nfeat = FEAT // LANES

    def prepare(picks_ref):
        def pick(c):
            return picks_ref[GRAM_ROWS - HALF + c * PANEL : GRAM_ROWS - HALF + (c + 1) * PANEL, :]

        acc_ref[...] = jnp.zeros_like(acc_ref)
        picked = jnp.concatenate([pick(c) for c in range(nfeat)], axis=1)
        pfac = jnp.concatenate([pick(nfeat + c) for c in range(NB)], axis=1)[:, :PREV]
        picked16 = picked.astype(BF16)
        picked_ref[...] = picked16
        high, low = split(pfac)
        pfac_ref[:PANEL, :] = high
        pfac_ref[PANEL:, :] = low
        square = picked * picked
        norm_row = mm(jnp.ones((8, FEAT), F32), square, NT, HIGHEST)[:1]
        norm_col = jnp.sum(square, axis=1, keepdims=True)
        norm_ref[...] = jnp.broadcast_to(norm_col, (PANEL, LANES))
        cross = mm(picked16, picked16, NT)
        dist = jnp.maximum(norm_col + norm_row - 2.0 * cross, 0.0)
        a = jnp.exp(-(2.0 / FEAT) * dist) - mm(pfac, pfac, NT, HIGHEST)
        sub = lax.broadcasted_iota(jnp.int32, (PANEL, PANEL), 0)
        lane = lax.broadcasted_iota(jnp.int32, (PANEL, PANEL), 1)
        b = jnp.where(sub == lane, 1.0, 0.0)
        for k in range(PANEL - 1):
            factor = jnp.where(sub > k, a[:, k : k + 1] / a[k : k + 1, k : k + 1], 0.0)
            a, b = a - factor * a[k : k + 1, :], b - factor * b[k : k + 1, :]
        pivot = jnp.sum(jnp.where(sub == lane, a, 0.0), axis=1, keepdims=True)
        inv_ref[...] = b / jnp.sqrt(pivot)

    @pl.when((step == 0) & (place_ref[1] == 1))
    def _():
        prepare(mine_ref)

    @pl.when((step == 0) & (place_ref[1] == 0))
    def _():
        prepare(other_ref)

    tile = samples_ref[...]
    squares = None
    for c in range(nfeat):
        part = tile[:, c * LANES : (c + 1) * LANES].astype(F32)
        squares = part * part if squares is None else squares + part * part
    norm = jnp.concatenate(
        [jnp.sum(squares[c : c + LANES].T, axis=0, keepdims=True) for c in range(0, PANEL_TILE, LANES)], axis=1
    )
    cross = mm(picked_ref[...], tile, NT)
    dist = jnp.maximum(norm + norm_ref[:, :1] - 2.0 * cross, 0.0)
    high, low = split(prev_ref[...])
    both = mm(pfac_ref[...], high, NN)
    inner = both[:PANEL] + (both[PANEL:] + mm(pfac_ref[:PANEL, :], low, NN))
    resid = jnp.exp(-(2.0 / FEAT) * dist) - inner
    new = mm(inv_ref[...], resid, NN, HIGHEST)
    new_ref[...] = new
    sub = lax.broadcasted_iota(jnp.int32, (EXT - PANEL, PANEL_TILE), 0)
    x = diag_ref[...] * jnp.concatenate([new, jnp.where(sub == 0, rhs_ref[...], 0.0)], axis=0)
    x = jnp.concatenate([x, jnp.zeros((48 - EXT, PANEL_TILE), F32)], axis=0)
    xh, xl = split(x)
    nh, nl = split(new)
    high, low = jnp.concatenate([high, nh], axis=0), jnp.concatenate([low, nl], axis=0)
    both = mm(jnp.concatenate([xh, xl], axis=0), high, NT)
    acc_ref[...] += both[:EXT] + (both[48 : 48 + EXT] + mm(xh, low, NT)[:EXT])

    @pl.when(step == ROWS // PANEL_TILE - 1)
    def _():
        for c in range(NB):
            ext_ref[EXT * c : EXT * (c + 1), :] = acc_ref[:, c * LANES : (c + 1) * LANES]
        ext_ref[EXT * NB :, :] = jnp.zeros((EXT_ROWS - EXT * NB, LANES), F32)


def panel(place, mine, other, diag, rhs, samples, prev_t):
    vec = pl.BlockSpec((1, PANEL_TILE), lambda i: (0, i))
    return pl.pallas_call(
        panel_kernel,
        grid=(ROWS // PANEL_TILE,),
        out_shape=(jax.ShapeDtypeStruct((PANEL, ROWS), F32), jax.ShapeDtypeStruct((EXT_ROWS, LANES), F32)),
        in_specs=[
            pl.BlockSpec(memory_space=pltpu.SMEM),
            pl.BlockSpec((HALF, LANES), whole),
            pl.BlockSpec((HALF, LANES), whole),
            vec,
            vec,
            pl.BlockSpec((PANEL_TILE, FEAT), lambda i: (i, 0)),
            pl.BlockSpec((PREV, PANEL_TILE), lambda i: (0, i)),
        ],
        out_specs=(pl.BlockSpec((PANEL, PANEL_TILE), lambda i: (0, i)), pl.BlockSpec((EXT_ROWS, LANES), whole)),
        scratch_shapes=[
            pltpu.VMEM((PANEL, FEAT), BF16),
            pltpu.VMEM((2 * PANEL, PREV), BF16),
            pltpu.VMEM((PANEL, LANES), F32),
            pltpu.VMEM((PANEL, PANEL), F32),
            pltpu.VMEM((EXT, RANK), F32),
        ],
        compiler_params=pltpu.CompilerParams(vmem_limit_bytes=VMEM_LIMIT),
        cost_estimate=pl.CostEstimate(flops=2 * ROWS * RANK * 1000, bytes_accessed=ROWS * (FEAT * 2 + PREV * 4), transcendentals=0),
        name="panel",
    )(place, mine, other, diag, rhs, samples, prev_t)


def inverse8(cols):
    sub = lax.broadcasted_iota(jnp.int32, (8, LANES), 0)

    def row(x, r):
        return jnp.broadcast_to(x[r : r + 1, :], (8, LANES))

    cols = list(cols)
    for k in range(0, 8, 2):
        a, b, c = row(cols[k], k), row(cols[k + 1], k), row(cols[k + 1], k + 1)
        scale = 1.0 / (a * c - b * b)
        ia, ib, ic = c * scale, -b * scale, a * scale
        ua = cols[k] * ia + cols[k + 1] * ib
        ub = cols[k] * ib + cols[k + 1] * ic
        keep = (sub != k) & (sub != k + 1)
        first = sub == k
        for m in range(8):
            if m in (k, k + 1):
                continue
            x, y = row(cols[m], k), row(cols[m], k + 1)
            cols[m] = jnp.where(keep, cols[m] - (ua * x + ub * y), jnp.where(first, ia * x + ib * y, ib * x + ic * y))
        cols[k] = jnp.where(keep, -ua, jnp.where(first, ia, ib))
        cols[k + 1] = jnp.where(keep, -ub, jnp.where(first, ib, ic))
    return cols


def tree(terms):
    while len(terms) > 1:
        terms = [a + b for a, b in zip(terms[::2], terms[1::2])]
    return terms[0]


def inverse128(rows):
    lane = lax.broadcasted_iota(jnp.int32, (8, LANES), 1)
    sub = lax.broadcasted_iota(jnp.int32, (8, LANES), 0)
    rows = list(rows)
    n = len(rows)

    def spread(x, at):
        return jnp.broadcast_to(x[:, at : at + 1], (8, LANES))

    for p in range(n):
        inside = (lane >= 8 * p) & (lane < 8 * p + 8)
        cols = inverse8([spread(rows[p], 8 * p + j) for j in range(8)])
        own = jnp.where(inside, jnp.where(lane == sub + 8 * p, 1.0, 0.0), rows[p])
        pivot = tree([cols[j] * jnp.broadcast_to(own[j : j + 1, :], (8, LANES)) for j in range(8)])
        spread_rows = [jnp.broadcast_to(pivot[j : j + 1, :], (8, LANES)) for j in range(8)]
        rows[p] = pivot
        for step in range(1, n):
            q = (p + step) % n
            update = tree([spread(rows[q], 8 * p + j) * spread_rows[j] for j in range(8)])
            rows[q] = jnp.where(inside, 0.0, rows[q]) - update
        yield
    return rows


EXTRA = EXT - PANEL


def left_parts(x):
    h, m, lo = three(x)
    return jnp.concatenate([h, m], axis=1), jnp.concatenate([h, lo], axis=1)


def right_parts(x, axis):
    h, m, lo = three(x)
    return tuple(jnp.concatenate(pair, axis=axis) for pair in ((h, h), (m, m), (lo, h)))


def product(left, right, dims):
    return mm(left[0], right[0], dims) + (mm(left[0], right[1], dims) + mm(left[1], right[2], dims))


def run(steps, fillers):
    count = LANES // 8
    done = 0
    for i in range(count + 1):
        try:
            next(steps)
        except StopIteration as end:
            for filler in fillers[done:]:
                filler()
            return end.value
        upto = len(fillers) * (i + 1) // count
        for filler in fillers[done:upto]:
            filler()
        done = upto


def eliminate(first, last, cols, t_refs, inv_ref):
    fillers = []
    for k in range(first, last):
        ref, at = cols[k]
        n = PACKED[k] - LANES
        block = run(inverse128([ref[at + 8 * i : at + 8 * i + 8, :] for i in range(LANES // 8)]), fillers)
        block = jnp.concatenate(block, axis=0)
        inv_ref[(k - first) * LANES : (k - first + 1) * LANES, :] = block
        weights = right_parts(block, 0)
        near = min(LANES, n)
        below = ref[at + LANES : at + LANES + near, :]
        right_near = right_parts(below, 1)
        times = product(left_parts(below), weights, NN)
        t_refs[k][:near, :] = times
        next_ref, next_at = cols[k + 1]
        next_ref[next_at : next_at + near, :near] -= product(left_parts(times), right_near, NT)
        fillers = []
        if n == near:
            continue
        far = {}

        def others(ref=ref, at=at, n=n, t_ref=t_refs[k], weights=weights, far=far):
            below = ref[at + 2 * LANES : at + LANES + n, :]
            times = product(left_parts(below), weights, NN)
            t_ref[LANES:, :] = times
            far["left"] = left_parts(times)
            far["right"] = right_parts(below, 1)

        def beside(ref=next_ref, at=next_at, n=n, far=far, right=right_near):
            ref[at + LANES : at + n, :] -= product(far["left"], right, NT)

        def update(j, k=k, n=n, far=far):
            r = (j - k - 2) * LANES
            wide = min(2 * LANES, n - LANES - r)
            value = product(tuple(x[r:] for x in far["left"]), tuple(x[r : r + wide] for x in far["right"]), NT)
            for c in range(0, wide, LANES):
                to_ref, to = cols[j + c // LANES]
                w = min(LANES, wide - c)
                to_ref[to : to + n - LANES - r - c, :w] -= value[c:, c : c + w]

        fillers = [others, beside] + [functools.partial(update, j) for j in range(k + 2, NB, 2)]
    for filler in fillers:
        filler()


CUTS = (0, 4, 7)
LEFT = [PACKED_AT[j] - PACKED_AT[CUTS[1]] for j in range(CUTS[1], NB + 1)]


def solve_first_kernel(place_ref, mine_ref, other_ref, left_ref, inv_ref, *refs):
    t_refs, a_ref = refs[:-1], refs[-1]
    lane = lax.broadcasted_iota(jnp.int32, (LANES, LANES), 1)
    sub = lax.broadcasted_iota(jnp.int32, (LANES, LANES), 0)

    def load(halves):
        for half, at, to, n in by_half(0, PACKED_AT[CUTS[1]]):
            a_ref[to : to + n, :] = halves[half][at : at + n, :]
        for half, at, to, n in by_half(PACKED_AT[CUTS[1]], GRAM_ROWS):
            left_ref[to : to + n, :] = halves[half][at : at + n, :]

    @pl.when(place_ref[1] == 0)
    def _():
        load((mine_ref, other_ref))

    @pl.when(place_ref[1] == 1)
    def _():
        load((other_ref, mine_ref))

    cols = [(a_ref, PACKED_AT[j]) for j in range(CUTS[1])] + [(left_ref, LEFT[j - CUTS[1]]) for j in range(CUTS[1], NB)]
    for j, (ref, at) in enumerate(cols):
        n = min(LANES, PACKED[j])
        ref[at : at + n, :] += jnp.where(lane == sub, 1.0, 0.0)[:n]
    eliminate(0, CUTS[1], cols, dict(enumerate(t_refs)), inv_ref)


def solve_second_kernel(left_ref, last_ref, inv_ref, *refs):
    t_refs, a_ref = refs[:-1], refs[-1]
    a_ref[...] = left_ref[...]
    eliminate(CUTS[1], CUTS[2], {j: (a_ref, LEFT[j - CUTS[1]]) for j in range(CUTS[1], NB)}, {CUTS[1] + i: r for i, r in enumerate(t_refs)}, inv_ref)
    last_ref[...] = a_ref[LEFT[-2] :, :]


def solve_last_kernel(last_ref, inv0_ref, inv1_ref, ext_ref, diag_ref, rhs_ref, new_ref, prev_any, *refs):
    t_refs, (out_ref, e_ref, w_ref, prev_ref, sem) = refs[: NB - 1], refs[NB - 1 :]
    step = PREV // 4
    copies = [pltpu.make_async_copy(prev_any.at[pl.ds(i * step, step)], prev_ref.at[pl.ds(i * step, step)], sem.at[i]) for i in range(4)]
    for copy in copies:
        copy.start()
    tail = PREV % LANES
    for j in range(NB):
        e_ref[:, j * LANES : (j + 1) * LANES] = ext_ref[EXT * j : EXT * (j + 1), :]
    scaled = []
    for k in range(NB - 1):
        here = e_ref[:, k * LANES : (k + 1) * LANES]
        left = left_parts(here)
        n = PACKED[k] - LANES
        change = product(left, right_parts(t_refs[k][...], 1), NT)
        e_ref[:, (k + 1) * LANES : PREV] -= change
        inv = inv0_ref[k * LANES : (k + 1) * LANES, :] if k < CUTS[1] else inv1_ref[(k - CUTS[1]) * LANES : (k - CUTS[1] + 1) * LANES, :]
        times = product(left, right_parts(inv, 0), NN)
        scaled.append(times)
        corner = product(left, right_parts(times, 1), NT)
        total = corner if k == 0 else total + corner
    lane = lax.broadcasted_iota(jnp.int32, (LANES, LANES), 1)
    sub = lax.broadcasted_iota(jnp.int32, (LANES, LANES), 0)
    shifted = jnp.concatenate([jnp.zeros((EXT, tail), F32), total[:, :PANEL]], axis=1)
    bottom = e_ref[:, (NB - 1) * LANES :] - shifted
    bottom = bottom + jnp.where(lax.broadcasted_iota(jnp.int32, (EXT, LANES), 1) == lax.broadcasted_iota(jnp.int32, (EXT, LANES), 0) + tail, 1.0, 0.0)
    block = jnp.concatenate([last_ref[...], bottom[:PANEL]], axis=0)
    block = jnp.where((lane >= tail) & (sub < tail), block.T, block)
    inverse = run(inverse128([block[8 * i : 8 * i + 8, :] for i in range(LANES // 8)]), [])
    inverse = jnp.concatenate(inverse, axis=0)
    value = mm(bottom[PANEL:], inverse, NN, HIGHEST)
    sums = [None] * (NB - 1)
    for k in reversed(range(1, NB)):
        spread = column(value[:1])
        w_ref[k * LANES : (k + 1) * LANES, :] = spread
        for j in range(k):
            r = (k - j - 1) * LANES
            rows = t_refs[j][r : r + min(LANES, PREV - k * LANES), :]
            if k == NB - 1:
                rows = jnp.concatenate([rows, scaled[j][:PANEL]], axis=0)
            part = (rows * spread).reshape(LANES // 8, 8, LANES).sum(axis=0)
            sums[j] = part if sums[j] is None else sums[j] + part
        value = scaled[k - 1][PANEL:] - jnp.sum(sums[k - 1], axis=0, keepdims=True)


    w_ref[:LANES, :] = column(value[:1])

    def weigh(ref, at, to):
        return ref[pl.ds(at, 8), :] * jnp.concatenate([w_ref[pl.ds(to, 8), :]] * (ROWS // LANES), axis=1)

    total = tree([weigh(new_ref, 8 * i, PREV + 8 * i) for i in range(PANEL // 8)])
    for copy in copies:
        copy.wait()

    def some(i, total):
        at = pl.multiple_of(i * 32, 32)
        return total + tree([weigh(prev_ref, at + 8 * j, at + 8 * j) for j in range(4)])

    total = lax.fori_loop(0, PREV // 32, some, total)
    fw = jnp.sum(total, axis=0, keepdims=True)
    out_ref[...] = diag_ref[...] * rhs_ref[...] - diag_ref[...] * fw


def block_spec(rows):
    return pl.BlockSpec((rows, LANES), whole)


def shape(rows):
    return jax.ShapeDtypeStruct((rows, LANES), F32)


def solve_first(place, mine, other):
    below = [PACKED[k] - LANES for k in range(CUTS[1])]
    outs = [LEFT[-1], CUTS[1] * LANES] + below
    return pl.pallas_call(
        solve_first_kernel,
        grid=(1,),
        out_shape=tuple(shape(r) for r in outs),
        in_specs=[pl.BlockSpec(memory_space=pltpu.SMEM), block_spec(HALF), block_spec(HALF)],
        out_specs=tuple(block_spec(r) for r in outs),
        scratch_shapes=[pltpu.VMEM((PACKED_AT[CUTS[1]], LANES), F32)],
        compiler_params=pltpu.CompilerParams(vmem_limit_bytes=VMEM_LIMIT),
        cost_estimate=pl.CostEstimate(flops=2 * 10**10, bytes_accessed=10**7, transcendentals=0),
        name="solve_first",
    )(place, mine, other)


def solve_second(left):
    below = [PACKED[k] - LANES for k in range(CUTS[1], CUTS[2])]
    outs = [PACKED[NB - 1], (CUTS[2] - CUTS[1]) * LANES] + below
    return pl.pallas_call(
        solve_second_kernel,
        grid=(1,),
        out_shape=tuple(shape(r) for r in outs),
        in_specs=[block_spec(LEFT[-1])],
        out_specs=tuple(block_spec(r) for r in outs),
        scratch_shapes=[pltpu.VMEM((LEFT[-1], LANES), F32)],
        compiler_params=pltpu.CompilerParams(vmem_limit_bytes=VMEM_LIMIT),
        cost_estimate=pl.CostEstimate(flops=2 * 10**10, bytes_accessed=10**7, transcendentals=0),
        name="solve_second",
    )(left)


def solve_last(last, inv0, inv1, ext, t, diag, rhs, new_t, prev_t):
    ins = [PACKED[NB - 1], CUTS[1] * LANES, (CUTS[2] - CUTS[1]) * LANES, EXT_ROWS]
    below = [PACKED[k] - LANES for k in range(NB - 1)]
    vec = pl.BlockSpec((1, ROWS), whole)
    return pl.pallas_call(
        solve_last_kernel,
        grid=(1,),
        out_shape=jax.ShapeDtypeStruct((1, ROWS), F32),
        in_specs=[block_spec(r) for r in ins]
        + [vec, vec, pl.BlockSpec((PANEL, ROWS), whole), pl.BlockSpec(memory_space=pl.ANY)]
        + [block_spec(r) for r in below],
        out_specs=vec,
        scratch_shapes=[
            pltpu.VMEM((EXT, RANK), F32),
            pltpu.VMEM((RANK, LANES), F32),
            pltpu.VMEM((PREV, ROWS), F32),
            pltpu.SemaphoreType.DMA((4,)),
        ],
        compiler_params=pltpu.CompilerParams(vmem_limit_bytes=VMEM_LIMIT),
        name="solve_last",
    )(last, inv0, inv1, ext, diag, rhs, new_t, prev_t, *t)


SAME_CORE = [[i for i in range(128) if i % 2 == core] for core in range(2)]
OTHER_CORE = [(i, i ^ 1) for i in range(128)]


def sum_large(keep, send):
    shape = keep.shape
    keep = (keep + lax.ppermute(send, AXES, OTHER_CORE)).reshape(64, -1, LANES)
    parts = lax.all_to_all(keep, AXES, 0, 0, axis_index_groups=SAME_CORE)
    part = jnp.sum(parts, axis=0)
    mine = lax.all_to_all(jnp.broadcast_to(part, parts.shape), AXES, 0, 0, axis_index_groups=SAME_CORE)
    mine = mine.reshape(shape)
    return mine, lax.ppermute(mine, AXES, OTHER_CORE)


def on_device(samples, prev_factor, pivots, inv_diag, rhs):
    index = lax.axis_index(AXES)
    place = jnp.stack([index * ROWS, index % 2]).astype(jnp.int32)
    diag, rhs = inv_diag.reshape(1, ROWS), rhs.reshape(1, ROWS)
    prev_t = prev_factor.T
    keep, send = gram(samples, prev_t, pivots, diag, place)
    mine, other = sum_large(keep, send)
    new_t, ext = panel(place, mine, other, diag, rhs, samples, prev_t)
    parts = lax.all_to_all(ext.reshape(128, -1, LANES), AXES, 0, 0)
    left, inv0, *t0 = solve_first(place, mine, other)
    parts, left = lax.optimization_barrier((parts, left))
    part = jnp.sum(parts, axis=0)
    ext = lax.all_to_all(jnp.broadcast_to(part, parts.shape), AXES, 0, 0).reshape(ext.shape)
    last, inv1, *t1 = solve_second(left)
    out = solve_last(last, inv0, inv1, ext, t0 + t1, diag, rhs, new_t, prev_t)
    return (new_t.T, out.reshape(ROWS))


def solution(mesh):
    return jax.shard_map(
        on_device,
        mesh=mesh,
        in_specs=(
            P(AXES, None),
            P(AXES, None),
            P(),
            P(AXES),
            P(AXES),
        ),
        out_specs=(P(AXES, None), P(AXES)),
        check_vma=False,
    )
```

```python
import functools

import jax
import jax.numpy as jnp
from jax import lax
from jax.experimental import pallas as pl
from jax.experimental.pallas import tpu as pltpu
from jax.sharding import PartitionSpec as P

FEAT = 2048
PREV = 992
PANEL = 32
RANK = 1024
ROWS = 2048
LANES = 128
NB = RANK // LANES
PACKED = [PREV - j * LANES for j in range(NB)]
PACKED_AT = [sum(PACKED[:j]) for j in range(NB + 1)]
GRAM_ROWS = PACKED_AT[NB]
PICK_ROWS = PANEL * (FEAT + RANK) // LANES
SEND_ROWS = GRAM_ROWS + PICK_ROWS
HALF = SEND_ROWS // 2
EXT = 40
EXT_ROWS = 512
HIGHEST = lax.Precision.HIGHEST
F32 = jnp.float32
BF16 = jnp.bfloat16
AXES = ("row", "col")
VMEM_LIMIT = 50 * 2**20


def split(x):
    high = x.astype(BF16)
    return high, (x - high.astype(F32)).astype(BF16)


def three(x):
    high = x.astype(BF16)
    rest = x - high.astype(F32)
    mid = rest.astype(BF16)
    return high, mid, (rest - mid.astype(F32)).astype(BF16)


def mm(a, b, dims, precision=None):
    return lax.dot_general(a, b, (dims, ((), ())), precision=precision, preferred_element_type=F32)


NN = ((1,), (0,))
NT = ((1,), (1,))
TN = ((0,), (0,))


def column(row):
    return jnp.broadcast_to(row, (LANES, LANES)).T


def whole(i):
    return (0, 0)


def by_half(start, stop):
    cuts = [start] + [HALF] * (start < HALF < stop) + [stop]
    return [(a // HALF, a % HALF, a - start, b - a) for a, b in zip(cuts, cuts[1:])]


GRAM_TILE = 1024


def gram_kernel(place_ref, diag_ref, samples_ref, prev_ref, keep_ref, send_ref, acc_ref, picks_ref, srow_ref, sem):
    step = pl.program_id(0)

    def row_copy(p):
        start = pl.multiple_of(place_ref[2 + p] // 16 * 16, 16)
        return pltpu.make_async_copy(samples_ref.at[pl.ds(start, 16)], srow_ref.at[p], sem.at[p])

    def owned(p):
        place = place_ref[2 + p]
        return (place >= 0) & (place < ROWS)

    @pl.when(step == 0)
    def _():
        acc_ref[...] = jnp.zeros_like(acc_ref)
        picks_ref[...] = jnp.zeros_like(picks_ref)

        def start(p, carry):
            @pl.when(owned(p))
            def _():
                row_copy(p).start()

            return carry

        lax.fori_loop(0, PANEL, start, 0)

    high, low = split(prev_ref[...] * jnp.sqrt(diag_ref[...]))
    at = 0
    for j in range(4):
        first = 256 * j
        wide = min(256, PREV - first)
        mine_h, mine_l = high[first : first + wide], low[first : first + wide]
        total = mm(high[first:], mine_h, NT) + (mm(high[first:], mine_l, NT) + mm(low[first:], mine_h, NT))
        acc_ref[at : at + PREV - first, :wide] += total
        at += PREV - first

    def factor_row(p, carry):
        place = place_ref[2 + p]

        @pl.when(owned(p) & (place // GRAM_TILE == step))
        def _():
            local = place % GRAM_TILE
            start = pl.multiple_of(local // LANES * LANES, LANES)
            chosen = lax.broadcasted_iota(jnp.int32, (16, LANES), 1) == local % LANES
            chosen = jnp.where(chosen, 1.0, 0.0).astype(BF16)
            parts = three(prev_ref[:, pl.ds(start, LANES)])
            row = (mm(chosen, parts[0], NT) + mm(chosen, parts[1], NT) + mm(chosen, parts[2], NT))[:1]
            to = PANEL * FEAT // LANES
            for c in range(NB - 1):
                picks_ref[pl.ds(to + c * PANEL + p, 1), :] = row[:, c * LANES : (c + 1) * LANES]
            picks_ref[pl.ds(to + (NB - 1) * PANEL + p, 1), : PREV % LANES] = row[:, (NB - 1) * LANES :]

        return carry

    lax.fori_loop(0, PANEL, factor_row, 0)

    @pl.when(step == ROWS // GRAM_TILE - 1)
    def _():
        def sample_row(p, carry):
            @pl.when(owned(p))
            def _():
                row_copy(p).wait()
                sub = lax.broadcasted_iota(jnp.int32, (16, FEAT), 0)
                row = jnp.sum(jnp.where(sub == place_ref[2 + p] % 16, srow_ref[p].astype(F32), 0.0), axis=0, keepdims=True)
                for c in range(FEAT // LANES):
                    picks_ref[pl.ds(c * PANEL + p, 1), :] = row[:, c * LANES : (c + 1) * LANES]

            return carry

        lax.fori_loop(0, PANEL, sample_row, 0)

        def write(halves):
            at = 0
            for j in range(NB):
                lane = (j % 2) * LANES
                wide = min(LANES, PREV - j * LANES)
                for half, to, skip, n in by_half(PACKED_AT[j], PACKED_AT[j + 1]):
                    halves[half][to : to + n, :wide] = acc_ref[at + lane + skip : at + lane + skip + n, lane : lane + wide]
                    if wide < LANES:
                        halves[half][to : to + n, wide:] = jnp.zeros((n, LANES - wide), F32)
                at += (PREV - j * LANES + LANES) * (j % 2)
            halves[1][GRAM_ROWS - HALF :, :] = picks_ref[...]

        @pl.when(place_ref[1] == 0)
        def _():
            write((keep_ref, send_ref))

        @pl.when(place_ref[1] == 1)
        def _():
            write((send_ref, keep_ref))


def gram(samples, prev_t, diag, place):
    half = jax.ShapeDtypeStruct((HALF, LANES), F32)
    return pl.pallas_call(
        gram_kernel,
        grid=(ROWS // GRAM_TILE,),
        out_shape=(half, half),
        in_specs=[
            pl.BlockSpec(memory_space=pltpu.SMEM),
            pl.BlockSpec((1, GRAM_TILE), lambda i: (0, i)),
            pl.BlockSpec(memory_space=pl.ANY),
            pl.BlockSpec((PREV, GRAM_TILE), lambda i: (0, i)),
        ],
        out_specs=(pl.BlockSpec((HALF, LANES), whole), pl.BlockSpec((HALF, LANES), whole)),
        scratch_shapes=[
            pltpu.VMEM((sum(PREV - 256 * j for j in range(4)), 256), F32),
            pltpu.VMEM((PICK_ROWS, LANES), F32),
            pltpu.VMEM((PANEL, 16, FEAT), BF16),
            pltpu.SemaphoreType.DMA((PANEL,)),
        ],
        compiler_params=pltpu.CompilerParams(vmem_limit_bytes=VMEM_LIMIT),
        cost_estimate=pl.CostEstimate(flops=6 * ROWS * RANK * 640, bytes_accessed=ROWS * PREV * 4, transcendentals=0),
        name="gram",
    )(place, diag, samples, prev_t)


PANEL_TILE = 512


def panel_kernel(place_ref, mine_ref, other_ref, diag_ref, rhs_ref, samples_ref, prev_ref, new_ref, ext_ref, picked_ref, pfac_ref, norm_ref, inv_ref, acc_ref):
    step = pl.program_id(0)
    nfeat = FEAT // LANES

    def prepare(picks_ref):
        def pick(c):
            return picks_ref[GRAM_ROWS - HALF + c * PANEL : GRAM_ROWS - HALF + (c + 1) * PANEL, :]

        acc_ref[...] = jnp.zeros_like(acc_ref)
        picked = jnp.concatenate([pick(c) for c in range(nfeat)], axis=1)
        pfac = jnp.concatenate([pick(nfeat + c) for c in range(NB)], axis=1)[:, :PREV]
        picked16 = picked.astype(BF16)
        picked_ref[...] = picked16
        high, low = split(pfac)
        pfac_ref[:PANEL, :] = high
        pfac_ref[PANEL:, :] = low
        square = picked * picked
        norm_row = mm(jnp.ones((8, FEAT), F32), square, NT, HIGHEST)[:1]
        norm_col = jnp.sum(square, axis=1, keepdims=True)
        norm_ref[...] = jnp.broadcast_to(norm_col, (PANEL, LANES))
        cross = mm(picked16, picked16, NT)
        dist = jnp.maximum(norm_col + norm_row - 2.0 * cross, 0.0)
        a = jnp.exp(-(2.0 / FEAT) * dist) - mm(pfac, pfac, NT, HIGHEST)
        sub = lax.broadcasted_iota(jnp.int32, (PANEL, PANEL), 0)
        lane = lax.broadcasted_iota(jnp.int32, (PANEL, PANEL), 1)
        b = jnp.where(sub == lane, 1.0, 0.0)
        for k in range(PANEL - 1):
            factor = jnp.where(sub > k, a[:, k : k + 1] / a[k : k + 1, k : k + 1], 0.0)
            a, b = a - factor * a[k : k + 1, :], b - factor * b[k : k + 1, :]
        pivot = jnp.sum(jnp.where(sub == lane, a, 0.0), axis=1, keepdims=True)
        inv_ref[...] = b / jnp.sqrt(pivot)

    @pl.when((step == 0) & (place_ref[1] == 1))
    def _():
        prepare(mine_ref)

    @pl.when((step == 0) & (place_ref[1] == 0))
    def _():
        prepare(other_ref)

    tile = samples_ref[...]
    squares = None
    for c in range(nfeat):
        part = tile[:, c * LANES : (c + 1) * LANES].astype(F32)
        squares = part * part if squares is None else squares + part * part
    norm = jnp.concatenate(
        [jnp.sum(squares[c : c + LANES].T, axis=0, keepdims=True) for c in range(0, PANEL_TILE, LANES)], axis=1
    )
    cross = mm(picked_ref[...], tile, NT)
    dist = jnp.maximum(norm + norm_ref[:, :1] - 2.0 * cross, 0.0)
    high, low = split(prev_ref[...])
    both = mm(pfac_ref[...], high, NN)
    inner = both[:PANEL] + (both[PANEL:] + mm(pfac_ref[:PANEL, :], low, NN))
    resid = jnp.exp(-(2.0 / FEAT) * dist) - inner
    new = mm(inv_ref[...], resid, NN, HIGHEST)
    new_ref[...] = new
    sub = lax.broadcasted_iota(jnp.int32, (EXT - PANEL, PANEL_TILE), 0)
    x = diag_ref[...] * jnp.concatenate([new, jnp.where(sub == 0, rhs_ref[...], 0.0)], axis=0)
    x = jnp.concatenate([x, jnp.zeros((48 - EXT, PANEL_TILE), F32)], axis=0)
    xh, xl = split(x)
    nh, nl = split(new)
    high, low = jnp.concatenate([high, nh], axis=0), jnp.concatenate([low, nl], axis=0)
    both = mm(jnp.concatenate([xh, xl], axis=0), high, NT)
    acc_ref[...] += both[:EXT] + (both[48 : 48 + EXT] + mm(xh, low, NT)[:EXT])

    @pl.when(step == ROWS // PANEL_TILE - 1)
    def _():
        for c in range(NB):
            ext_ref[EXT * c : EXT * (c + 1), :] = acc_ref[:, c * LANES : (c + 1) * LANES]
        ext_ref[EXT * NB :, :] = jnp.zeros((EXT_ROWS - EXT * NB, LANES), F32)


def panel(place, mine, other, diag, rhs, samples, prev_t):
    vec = pl.BlockSpec((1, PANEL_TILE), lambda i: (0, i))
    return pl.pallas_call(
        panel_kernel,
        grid=(ROWS // PANEL_TILE,),
        out_shape=(jax.ShapeDtypeStruct((PANEL, ROWS), F32), jax.ShapeDtypeStruct((EXT_ROWS, LANES), F32)),
        in_specs=[
            pl.BlockSpec(memory_space=pltpu.SMEM),
            pl.BlockSpec((HALF, LANES), whole),
            pl.BlockSpec((HALF, LANES), whole),
            vec,
            vec,
            pl.BlockSpec((PANEL_TILE, FEAT), lambda i: (i, 0)),
            pl.BlockSpec((PREV, PANEL_TILE), lambda i: (0, i)),
        ],
        out_specs=(pl.BlockSpec((PANEL, PANEL_TILE), lambda i: (0, i)), pl.BlockSpec((EXT_ROWS, LANES), whole)),
        scratch_shapes=[
            pltpu.VMEM((PANEL, FEAT), BF16),
            pltpu.VMEM((2 * PANEL, PREV), BF16),
            pltpu.VMEM((PANEL, LANES), F32),
            pltpu.VMEM((PANEL, PANEL), F32),
            pltpu.VMEM((EXT, RANK), F32),
        ],
        compiler_params=pltpu.CompilerParams(vmem_limit_bytes=VMEM_LIMIT),
        cost_estimate=pl.CostEstimate(flops=2 * ROWS * RANK * 1000, bytes_accessed=ROWS * (FEAT * 2 + PREV * 4), transcendentals=0),
        name="panel",
    )(place, mine, other, diag, rhs, samples, prev_t)


def inverse8(cols):
    sub = lax.broadcasted_iota(jnp.int32, (8, LANES), 0)

    def row(x, r):
        return jnp.broadcast_to(x[r : r + 1, :], (8, LANES))

    cols = list(cols)
    for k in range(0, 8, 2):
        a, b, c = row(cols[k], k), row(cols[k + 1], k), row(cols[k + 1], k + 1)
        scale = 1.0 / (a * c - b * b)
        ia, ib, ic = c * scale, -b * scale, a * scale
        ua = cols[k] * ia + cols[k + 1] * ib
        ub = cols[k] * ib + cols[k + 1] * ic
        keep = (sub != k) & (sub != k + 1)
        first = sub == k
        for m in range(8):
            if m in (k, k + 1):
                continue
            x, y = row(cols[m], k), row(cols[m], k + 1)
            cols[m] = jnp.where(keep, cols[m] - (ua * x + ub * y), jnp.where(first, ia * x + ib * y, ib * x + ic * y))
        cols[k] = jnp.where(keep, -ua, jnp.where(first, ia, ib))
        cols[k + 1] = jnp.where(keep, -ub, jnp.where(first, ib, ic))
    return cols


def tree(terms):
    while len(terms) > 1:
        terms = [a + b for a, b in zip(terms[::2], terms[1::2])]
    return terms[0]


def inverse128(rows):
    lane = lax.broadcasted_iota(jnp.int32, (8, LANES), 1)
    sub = lax.broadcasted_iota(jnp.int32, (8, LANES), 0)
    rows = list(rows)
    n = len(rows)

    def spread(x, at):
        return jnp.broadcast_to(x[:, at : at + 1], (8, LANES))

    for p in range(n):
        inside = (lane >= 8 * p) & (lane < 8 * p + 8)
        cols = inverse8([spread(rows[p], 8 * p + j) for j in range(8)])
        own = jnp.where(inside, jnp.where(lane == sub + 8 * p, 1.0, 0.0), rows[p])
        pivot = tree([cols[j] * jnp.broadcast_to(own[j : j + 1, :], (8, LANES)) for j in range(8)])
        times = jnp.where(inside, 0.0, jnp.where(lane < 8 * p, -rows[p], rows[p]))
        if p + 1 < n:
            update = tree([spread(rows[p + 1], 8 * p + j) * jnp.broadcast_to(pivot[j : j + 1, :], (8, LANES)) for j in range(8)])
            following = jnp.where(inside, 0.0, rows[p + 1]) - update
        h, m, lo = (x.astype(F32) for x in three(times))
        ph, pm, plo = (x.astype(F32) for x in three(pivot))
        left = jnp.concatenate([h, h, m, m, h, lo], axis=0).astype(BF16)
        right = jnp.concatenate([ph, pm, ph, pm, plo, ph], axis=0).astype(BF16)
        update = mm(left, right, TN)
        for q in range(n):
            if q not in (p, p + 1):
                rows[q] = jnp.where(inside, 0.0, rows[q]) - update[8 * q : 8 * q + 8]
        rows[p] = pivot
        if p + 1 < n:
            rows[p + 1] = following
        yield
    return rows


EXTRA = EXT - PANEL


def left_parts(x):
    h, m, lo = three(x)
    return jnp.concatenate([h, m], axis=1), jnp.concatenate([h, lo], axis=1)


def right_parts(x, axis):
    h, m, lo = three(x)
    return tuple(jnp.concatenate(pair, axis=axis) for pair in ((h, h), (m, m), (lo, h)))


def product(left, right, dims):
    return mm(left[0], right[0], dims) + (mm(left[0], right[1], dims) + mm(left[1], right[2], dims))


def run(steps, fillers):
    count = LANES // 8
    done = 0
    for i in range(count + 1):
        try:
            next(steps)
        except StopIteration as end:
            for filler in fillers[done:]:
                filler()
            return end.value
        upto = len(fillers) * (i + 1) // count
        for filler in fillers[done:upto]:
            filler()
        done = upto


def eliminate(first, last, cols, t_refs, inv_ref):
    fillers = []
    for k in range(first, last):
        ref, at = cols[k]
        n = PACKED[k] - LANES
        block = run(inverse128([ref[at + 8 * i : at + 8 * i + 8, :] for i in range(LANES // 8)]), fillers)
        block = jnp.concatenate(block, axis=0)
        inv_ref[(k - first) * LANES : (k - first + 1) * LANES, :] = block
        weights = right_parts(block, 0)
        near = min(LANES, n)
        below = ref[at + LANES : at + LANES + near, :]
        right_near = right_parts(below, 1)
        times = product(left_parts(below), weights, NN)
        t_refs[k][:near, :] = times
        next_ref, next_at = cols[k + 1]
        next_ref[next_at : next_at + near, :near] -= product(left_parts(times), right_near, NT)
        fillers = []
        if n == near:
            continue
        far = {}

        def others(ref=ref, at=at, n=n, t_ref=t_refs[k], weights=weights, far=far):
            below = ref[at + 2 * LANES : at + LANES + n, :]
            times = product(left_parts(below), weights, NN)
            t_ref[LANES:, :] = times
            far["left"] = left_parts(times)
            far["right"] = right_parts(below, 1)

        def beside(ref=next_ref, at=next_at, n=n, far=far, right=right_near):
            ref[at + LANES : at + n, :] -= product(far["left"], right, NT)

        def update(j, k=k, n=n, far=far):
            r = (j - k - 2) * LANES
            wide = min(2 * LANES, n - LANES - r)
            value = product(tuple(x[r:] for x in far["left"]), tuple(x[r : r + wide] for x in far["right"]), NT)
            for c in range(0, wide, LANES):
                to_ref, to = cols[j + c // LANES]
                w = min(LANES, wide - c)
                to_ref[to : to + n - LANES - r - c, :w] -= value[c:, c : c + w]

        fillers = [others, beside] + [functools.partial(update, j) for j in range(k + 2, NB, 2)]
    for filler in fillers:
        filler()


CUTS = (0, 4, 7)
LEFT = [PACKED_AT[j] - PACKED_AT[CUTS[1]] for j in range(CUTS[1], NB + 1)]


def solve_first_kernel(place_ref, mine_ref, other_ref, left_ref, inv_ref, token_ref, *refs):
    token_ref[...] = jnp.zeros_like(token_ref)
    t_refs, a_ref = refs[:-1], refs[-1]
    lane = lax.broadcasted_iota(jnp.int32, (LANES, LANES), 1)
    sub = lax.broadcasted_iota(jnp.int32, (LANES, LANES), 0)

    def load(halves):
        for half, at, to, n in by_half(0, PACKED_AT[CUTS[1]]):
            a_ref[to : to + n, :] = halves[half][at : at + n, :]
        for half, at, to, n in by_half(PACKED_AT[CUTS[1]], GRAM_ROWS):
            left_ref[to : to + n, :] = halves[half][at : at + n, :]

    @pl.when(place_ref[1] == 0)
    def _():
        load((mine_ref, other_ref))

    @pl.when(place_ref[1] == 1)
    def _():
        load((other_ref, mine_ref))

    cols = [(a_ref, PACKED_AT[j]) for j in range(CUTS[1])] + [(left_ref, LEFT[j - CUTS[1]]) for j in range(CUTS[1], NB)]
    for j, (ref, at) in enumerate(cols):
        n = min(LANES, PACKED[j])
        ref[at : at + n, :] += jnp.where(lane == sub, 1.0, 0.0)[:n]
    eliminate(0, CUTS[1], cols, dict(enumerate(t_refs)), inv_ref)


def solve_second_kernel(token_ref, left_ref, last_ref, inv_ref, *refs):
    t_refs, a_ref = refs[:-1], refs[-1]
    a_ref[...] = left_ref[...]
    eliminate(CUTS[1], CUTS[2], {j: (a_ref, LEFT[j - CUTS[1]]) for j in range(CUTS[1], NB)}, {CUTS[1] + i: r for i, r in enumerate(t_refs)}, inv_ref)
    last_ref[...] = a_ref[LEFT[-2] :, :]


def solve_last_kernel(last_ref, inv0_ref, inv1_ref, ext_ref, diag_ref, rhs_ref, new_ref, prev_any, *refs):
    t_refs, (out_ref, e_ref, w_ref, prev_ref, sem) = refs[: NB - 1], refs[NB - 1 :]
    step = PREV // 4
    copies = [pltpu.make_async_copy(prev_any.at[pl.ds(i * step, step)], prev_ref.at[pl.ds(i * step, step)], sem.at[i]) for i in range(4)]
    for copy in copies:
        copy.start()
    tail = PREV % LANES
    for j in range(NB):
        e_ref[:, j * LANES : (j + 1) * LANES] = ext_ref[EXT * j : EXT * (j + 1), :]
    scaled = []
    for k in range(NB - 1):
        here = e_ref[:, k * LANES : (k + 1) * LANES]
        left = left_parts(here)
        n = PACKED[k] - LANES
        change = product(left, right_parts(t_refs[k][...], 1), NT)
        e_ref[:, (k + 1) * LANES : PREV] -= change
        inv = inv0_ref[k * LANES : (k + 1) * LANES, :] if k < CUTS[1] else inv1_ref[(k - CUTS[1]) * LANES : (k - CUTS[1] + 1) * LANES, :]
        times = product(left, right_parts(inv, 0), NN)
        scaled.append(times)
        corner = product(left, right_parts(times, 1), NT)
        total = corner if k == 0 else total + corner
    lane = lax.broadcasted_iota(jnp.int32, (LANES, LANES), 1)
    sub = lax.broadcasted_iota(jnp.int32, (LANES, LANES), 0)
    shifted = jnp.concatenate([jnp.zeros((EXT, tail), F32), total[:, :PANEL]], axis=1)
    bottom = e_ref[:, (NB - 1) * LANES :] - shifted
    bottom = bottom + jnp.where(lax.broadcasted_iota(jnp.int32, (EXT, LANES), 1) == lax.broadcasted_iota(jnp.int32, (EXT, LANES), 0) + tail, 1.0, 0.0)
    block = jnp.concatenate([last_ref[...], bottom[:PANEL]], axis=0)
    block = jnp.where((lane >= tail) & (sub < tail), block.T, block)
    inverse = run(inverse128([block[8 * i : 8 * i + 8, :] for i in range(LANES // 8)]), [])
    inverse = jnp.concatenate(inverse, axis=0)
    value = mm(bottom[PANEL:], inverse, NN, HIGHEST)
    sums = [None] * (NB - 1)
    for k in reversed(range(1, NB)):
        spread = column(value[:1])
        w_ref[k * LANES : (k + 1) * LANES, :] = spread
        for j in range(k):
            r = (k - j - 1) * LANES
            rows = t_refs[j][r : r + min(LANES, PREV - k * LANES), :]
            if k == NB - 1:
                rows = jnp.concatenate([rows, scaled[j][:PANEL]], axis=0)
            part = (rows * spread).reshape(LANES // 8, 8, LANES).sum(axis=0)
            sums[j] = part if sums[j] is None else sums[j] + part
        value = scaled[k - 1][PANEL:] - jnp.sum(sums[k - 1], axis=0, keepdims=True)


    w_ref[:LANES, :] = column(value[:1])

    def weigh(ref, at, to):
        return ref[pl.ds(at, 8), :] * jnp.concatenate([w_ref[pl.ds(to, 8), :]] * (ROWS // LANES), axis=1)

    total = tree([weigh(new_ref, 8 * i, PREV + 8 * i) for i in range(PANEL // 8)])
    for copy in copies:
        copy.wait()

    for i in range(0, PREV, 32):
        total = total + tree([weigh(prev_ref, i + 8 * j, i + 8 * j) for j in range(4)])
    fw = jnp.sum(total, axis=0, keepdims=True)
    out_ref[...] = diag_ref[...] * rhs_ref[...] - diag_ref[...] * fw


def block_spec(rows):
    return pl.BlockSpec((rows, LANES), whole)


def shape(rows):
    return jax.ShapeDtypeStruct((rows, LANES), F32)


def solve_first(place, mine, other):
    below = [PACKED[k] - LANES for k in range(CUTS[1])]
    outs = [LEFT[-1], CUTS[1] * LANES, 8] + below
    return pl.pallas_call(
        solve_first_kernel,
        grid=(1,),
        out_shape=tuple(shape(r) for r in outs),
        in_specs=[pl.BlockSpec(memory_space=pltpu.SMEM), block_spec(HALF), block_spec(HALF)],
        out_specs=tuple(block_spec(r) for r in outs),
        scratch_shapes=[pltpu.VMEM((PACKED_AT[CUTS[1]], LANES), F32)],
        compiler_params=pltpu.CompilerParams(vmem_limit_bytes=VMEM_LIMIT),
        cost_estimate=pl.CostEstimate(flops=2 * 10**10, bytes_accessed=10**7, transcendentals=0),
        name="solve_first",
    )(place, mine, other)


def solve_second(token, left):
    below = [PACKED[k] - LANES for k in range(CUTS[1], CUTS[2])]
    outs = [PACKED[NB - 1], (CUTS[2] - CUTS[1]) * LANES] + below
    return pl.pallas_call(
        solve_second_kernel,
        grid=(1,),
        out_shape=tuple(shape(r) for r in outs),
        in_specs=[pl.BlockSpec(memory_space=pl.ANY), block_spec(LEFT[-1])],
        out_specs=tuple(block_spec(r) for r in outs),
        scratch_shapes=[pltpu.VMEM((LEFT[-1], LANES), F32)],
        compiler_params=pltpu.CompilerParams(vmem_limit_bytes=VMEM_LIMIT),
        cost_estimate=pl.CostEstimate(flops=2 * 10**10, bytes_accessed=10**7, transcendentals=0),
        name="solve_second",
    )(token, left)


def solve_last(last, inv0, inv1, ext, t, diag, rhs, new_t, prev_t):
    ins = [PACKED[NB - 1], CUTS[1] * LANES, (CUTS[2] - CUTS[1]) * LANES, EXT_ROWS]
    below = [PACKED[k] - LANES for k in range(NB - 1)]
    vec = pl.BlockSpec((1, ROWS), whole)
    return pl.pallas_call(
        solve_last_kernel,
        grid=(1,),
        out_shape=jax.ShapeDtypeStruct((1, ROWS), F32),
        in_specs=[block_spec(r) for r in ins]
        + [vec, vec, pl.BlockSpec((PANEL, ROWS), whole), pl.BlockSpec(memory_space=pl.ANY)]
        + [block_spec(r) for r in below],
        out_specs=vec,
        scratch_shapes=[
            pltpu.VMEM((EXT, RANK), F32),
            pltpu.VMEM((RANK, LANES), F32),
            pltpu.VMEM((PREV, ROWS), F32),
            pltpu.SemaphoreType.DMA((4,)),
        ],
        compiler_params=pltpu.CompilerParams(vmem_limit_bytes=VMEM_LIMIT),
        name="solve_last",
    )(last, inv0, inv1, ext, diag, rhs, new_t, prev_t, *t)


SAME_CORE = [[i for i in range(128) if i % 2 == core] for core in range(2)]
OTHER_CORE = [(i, i ^ 1) for i in range(128)]


def sum_large(keep, send):
    shape = keep.shape
    keep = (keep + lax.ppermute(send, AXES, OTHER_CORE)).reshape(64, -1, LANES)
    parts = lax.all_to_all(keep, AXES, 0, 0, axis_index_groups=SAME_CORE)
    part = jnp.sum(parts, axis=0)
    mine = lax.all_to_all(jnp.broadcast_to(part, parts.shape), AXES, 0, 0, axis_index_groups=SAME_CORE)
    mine = mine.reshape(shape)
    return mine, lax.ppermute(mine, AXES, OTHER_CORE)


def on_device(samples, prev_factor, pivots, inv_diag, rhs):
    index = lax.axis_index(AXES)
    place = jnp.concatenate([jnp.stack([index, index % 2]), pivots - index * ROWS]).astype(jnp.int32)
    diag, rhs = inv_diag.reshape(1, ROWS), rhs.reshape(1, ROWS)
    prev_t = prev_factor.T
    keep, send = gram(samples, prev_t, diag, place)
    mine, other = sum_large(keep, send)
    new_t, ext = panel(place, mine, other, diag, rhs, samples, prev_t)
    parts = lax.all_to_all(ext.reshape(128, -1, LANES), AXES, 0, 0)
    left, inv0, token, *t0 = solve_first(place, mine, other)
    parts, token = lax.optimization_barrier((parts, token))
    part = jnp.sum(parts, axis=0)
    ext = lax.all_to_all(jnp.broadcast_to(part, parts.shape), AXES, 0, 0).reshape(ext.shape)
    last, inv1, *t1 = solve_second(token, left)
    out = solve_last(last, inv0, inv1, ext, t0 + t1, diag, rhs, new_t, prev_t)
    return (new_t.T, out.reshape(ROWS))


def solution(mesh):
    return jax.shard_map(
        on_device,
        mesh=mesh,
        in_specs=(
            P(AXES, None),
            P(AXES, None),
            P(),
            P(AXES),
            P(AXES),
        ),
        out_specs=(P(AXES, None), P(AXES)),
        check_vma=False,
    )
```

```python
import functools

import jax
import jax.numpy as jnp
from jax import lax
from jax.experimental import pallas as pl
from jax.experimental.pallas import tpu as pltpu
from jax.sharding import PartitionSpec as P

FEAT = 2048
PREV = 992
PANEL = 32
RANK = 1024
ROWS = 2048
LANES = 128
NB = RANK // LANES
PACKED = [PREV - j * LANES for j in range(NB)]
PACKED_AT = [sum(PACKED[:j]) for j in range(NB + 1)]
GRAM_ROWS = PACKED_AT[NB]
PICK_ROWS = PANEL * (FEAT + RANK) // LANES
SEND_ROWS = GRAM_ROWS + PICK_ROWS
HALF = SEND_ROWS // 2
EXT = 40
EXT_ROWS = 512
HIGHEST = lax.Precision.HIGHEST
F32 = jnp.float32
BF16 = jnp.bfloat16
AXES = ("row", "col")
VMEM_LIMIT = 50 * 2**20


def split(x):
    high = x.astype(BF16)
    return high, (x - high.astype(F32)).astype(BF16)


def three(x):
    high = x.astype(BF16)
    rest = x - high.astype(F32)
    mid = rest.astype(BF16)
    return high, mid, (rest - mid.astype(F32)).astype(BF16)


def mm(a, b, dims, precision=None):
    return lax.dot_general(a, b, (dims, ((), ())), precision=precision, preferred_element_type=F32)


NN = ((1,), (0,))
NT = ((1,), (1,))
TN = ((0,), (0,))


def column(row):
    return jnp.broadcast_to(row, (LANES, LANES)).T


def whole(i):
    return (0, 0)


def by_half(start, stop):
    cuts = [start] + [HALF] * (start < HALF < stop) + [stop]
    return [(a // HALF, a % HALF, a - start, b - a) for a, b in zip(cuts, cuts[1:])]


GRAM_TILE = 512


def gram_kernel(place_ref, diag_ref, samples_ref, prev_any, keep_ref, send_ref, acc_ref, picks_ref, srow_ref, prev_ref, sem, tile_sem):
    tiles = ROWS // GRAM_TILE
    copies = []
    for i in range(tiles):
        here = pl.ds(i * GRAM_TILE, GRAM_TILE)
        copies.append(pltpu.make_async_copy(prev_any.at[:, here], prev_ref.at[:, here], tile_sem.at[i]))
        copies[i].start()

    def row_copy(p):
        start = pl.multiple_of(place_ref[2 + p] // 16 * 16, 16)
        return pltpu.make_async_copy(samples_ref.at[pl.ds(start, 16)], srow_ref.at[p], sem.at[p])

    def owned(p):
        place = place_ref[2 + p]
        return (place >= 0) & (place < ROWS)

    picks_ref[...] = jnp.zeros_like(picks_ref)

    def start(p, carry):
        @pl.when(owned(p))
        def _():
            row_copy(p).start()

        return carry

    lax.fori_loop(0, PANEL, start, 0)

    for i in range(tiles):
        copies[i].wait()
        here = slice(i * GRAM_TILE, (i + 1) * GRAM_TILE)
        high, low = split(prev_ref[:, here] * jnp.sqrt(diag_ref[:, here]))
        at = 0
        for j in range(4):
            first = 256 * j
            wide = min(256, PREV - first)
            mine_h, mine_l = high[first : first + wide], low[first : first + wide]
            total = mm(high[first:], mine_h, NT) + (mm(high[first:], mine_l, NT) + mm(low[first:], mine_h, NT))
            if i > 0:
                total = total + acc_ref[at : at + PREV - first, :wide]
            acc_ref[at : at + PREV - first, :wide] = total
            at += PREV - first

    def factor_row(p, carry):
        place = place_ref[2 + p]

        @pl.when(owned(p))
        def _():
            start = pl.multiple_of(place // LANES * LANES, LANES)
            chosen = lax.broadcasted_iota(jnp.int32, (16, LANES), 1) == place % LANES
            chosen = jnp.where(chosen, 1.0, 0.0).astype(BF16)
            parts = three(prev_ref[:, pl.ds(start, LANES)])
            row = (mm(chosen, parts[0], NT) + mm(chosen, parts[1], NT) + mm(chosen, parts[2], NT))[:1]
            to = PANEL * FEAT // LANES
            for c in range(NB - 1):
                picks_ref[pl.ds(to + c * PANEL + p, 1), :] = row[:, c * LANES : (c + 1) * LANES]
            picks_ref[pl.ds(to + (NB - 1) * PANEL + p, 1), : PREV % LANES] = row[:, (NB - 1) * LANES :]

        return carry

    lax.fori_loop(0, PANEL, factor_row, 0)

    def sample_row(p, carry):
        @pl.when(owned(p))
        def _():
            row_copy(p).wait()
            sub = lax.broadcasted_iota(jnp.int32, (16, FEAT), 0)
            row = jnp.sum(jnp.where(sub == place_ref[2 + p] % 16, srow_ref[p].astype(F32), 0.0), axis=0, keepdims=True)
            for c in range(FEAT // LANES):
                picks_ref[pl.ds(c * PANEL + p, 1), :] = row[:, c * LANES : (c + 1) * LANES]

        return carry

    lax.fori_loop(0, PANEL, sample_row, 0)

    def write(halves):
        at = 0
        for j in range(NB):
            lane = (j % 2) * LANES
            wide = min(LANES, PREV - j * LANES)
            for half, to, skip, n in by_half(PACKED_AT[j], PACKED_AT[j + 1]):
                halves[half][to : to + n, :wide] = acc_ref[at + lane + skip : at + lane + skip + n, lane : lane + wide]
                if wide < LANES:
                    halves[half][to : to + n, wide:] = jnp.zeros((n, LANES - wide), F32)
            at += (PREV - j * LANES + LANES) * (j % 2)
        halves[1][GRAM_ROWS - HALF :, :] = picks_ref[...]

    @pl.when(place_ref[1] == 0)
    def _():
        write((keep_ref, send_ref))

    @pl.when(place_ref[1] == 1)
    def _():
        write((send_ref, keep_ref))


def gram(samples, prev_t, diag, place):
    half = jax.ShapeDtypeStruct((HALF, LANES), F32)
    return pl.pallas_call(
        gram_kernel,
        grid=(1,),
        out_shape=(half, half),
        in_specs=[
            pl.BlockSpec(memory_space=pltpu.SMEM),
            pl.BlockSpec((1, ROWS), whole),
            pl.BlockSpec(memory_space=pl.ANY),
            pl.BlockSpec(memory_space=pl.ANY),
        ],
        out_specs=(pl.BlockSpec((HALF, LANES), whole), pl.BlockSpec((HALF, LANES), whole)),
        scratch_shapes=[
            pltpu.VMEM((sum(PREV - 256 * j for j in range(4)), 256), F32),
            pltpu.VMEM((PICK_ROWS, LANES), F32),
            pltpu.VMEM((PANEL, 16, FEAT), BF16),
            pltpu.VMEM((PREV, ROWS), F32),
            pltpu.SemaphoreType.DMA((PANEL,)),
            pltpu.SemaphoreType.DMA((ROWS // GRAM_TILE,)),
        ],
        compiler_params=pltpu.CompilerParams(vmem_limit_bytes=VMEM_LIMIT),
        cost_estimate=pl.CostEstimate(flops=6 * ROWS * RANK * 640, bytes_accessed=ROWS * PREV * 4, transcendentals=0),
        name="gram",
    )(place, diag, samples, prev_t)


PANEL_TILE = 512


def panel_kernel(place_ref, mine_ref, other_ref, diag_ref, rhs_ref, samples_any, prev_any, new_ref, ext_ref, picked_ref, pfac_ref, norm_ref, block_ref, samples_ref, prev_ref, sem):
    tiles = ROWS // PANEL_TILE
    copies = []
    for i in range(tiles):
        rows = pl.ds(i * PANEL_TILE, PANEL_TILE)
        copies.append(pltpu.make_async_copy(samples_any.at[rows], samples_ref.at[rows], sem.at[0, i]))
        copies.append(pltpu.make_async_copy(prev_any.at[:, rows], prev_ref.at[:, rows], sem.at[1, i]))
    for copy in copies:
        copy.start()
    nfeat = FEAT // LANES

    def prepare(picks_ref):
        def pick(c):
            return picks_ref[GRAM_ROWS - HALF + c * PANEL : GRAM_ROWS - HALF + (c + 1) * PANEL, :]

        picked = jnp.concatenate([pick(c) for c in range(nfeat)], axis=1)
        pfac = jnp.concatenate([pick(nfeat + c) for c in range(NB)], axis=1)[:, :PREV]
        picked16 = picked.astype(BF16)
        picked_ref[...] = picked16
        high, low = split(pfac)
        pfac_ref[:PANEL, :] = high
        pfac_ref[PANEL:, :] = low
        square = picked * picked
        norm_row = mm(jnp.ones((8, FEAT), F32), square, NT, HIGHEST)[:1]
        norm_col = jnp.sum(square, axis=1, keepdims=True)
        norm_ref[...] = jnp.broadcast_to(norm_col, (PANEL, LANES))
        cross = mm(picked16, picked16, NT)
        dist = jnp.maximum(norm_col + norm_row - 2.0 * cross, 0.0)
        block_ref[...] = jnp.exp(-(2.0 / FEAT) * dist) - mm(pfac, pfac, NT, HIGHEST)

    @pl.when(place_ref[1] == 1)
    def _():
        prepare(mine_ref)

    @pl.when(place_ref[1] == 0)
    def _():
        prepare(other_ref)

    def residual(i):
        copies[2 * i].wait()
        copies[2 * i + 1].wait()
        tile = samples_ref[i * PANEL_TILE : (i + 1) * PANEL_TILE, :]
        squares = None
        for c in range(nfeat):
            part = tile[:, c * LANES : (c + 1) * LANES].astype(F32)
            squares = part * part if squares is None else squares + part * part
        norm = jnp.concatenate(
            [jnp.sum(squares[c : c + LANES].T, axis=0, keepdims=True) for c in range(0, PANEL_TILE, LANES)], axis=1
        )
        cross = mm(picked_ref[...], tile, NT)
        dist = jnp.maximum(norm + norm_ref[:, :1] - 2.0 * cross, 0.0)
        high, low = split(prev_ref[:, i * PANEL_TILE : (i + 1) * PANEL_TILE])
        both = mm(pfac_ref[...], high, NN)
        inner = both[:PANEL] + (both[PANEL:] + mm(pfac_ref[:PANEL, :], low, NN))
        return jnp.exp(-(2.0 / FEAT) * dist) - inner, high, low

    def products(i, inverse, resid, high, low):
        h, m, lo = three(resid)
        new = mm(inverse, jnp.concatenate([h, m, h, m, lo, h], axis=0), NN)
        here = slice(i * PANEL_TILE, (i + 1) * PANEL_TILE)
        new_ref[:, here] = new
        sub = lax.broadcasted_iota(jnp.int32, (EXT - PANEL, PANEL_TILE), 0)
        x = diag_ref[:, here] * jnp.concatenate([new, jnp.where(sub == 0, rhs_ref[:, here], 0.0)], axis=0)
        x = jnp.concatenate([x, jnp.zeros((48 - EXT, PANEL_TILE), F32)], axis=0)
        xh, xl = split(x)
        nh, nl = split(new)
        high, low = jnp.concatenate([high, nh], axis=0), jnp.concatenate([low, nl], axis=0)
        both = mm(jnp.concatenate([xh, xl], axis=0), high, NT)
        return both[:EXT] + (both[48 : 48 + EXT] + mm(xh, low, NT)[:EXT])

    first = residual(0)
    a = block_ref[...]
    sub = lax.broadcasted_iota(jnp.int32, (PANEL, PANEL), 0)
    lane = lax.broadcasted_iota(jnp.int32, (PANEL, PANEL), 1)
    b = jnp.where(sub == lane, 1.0, 0.0)
    for k in range(PANEL - 1):
        factor = jnp.where(sub > k, a[:, k : k + 1] / a[k : k + 1, k : k + 1], 0.0)
        a, b = a - factor * a[k : k + 1, :], b - factor * b[k : k + 1, :]
    pivot = jnp.sum(jnp.where(sub == lane, a, 0.0), axis=1, keepdims=True)
    h, m, lo = (x.astype(F32) for x in three(b / jnp.sqrt(pivot)))
    inverse = jnp.concatenate([h, h, m, m, h, lo], axis=1).astype(BF16)
    total = products(0, inverse, *first)
    for i in range(1, tiles):
        total = total + products(i, inverse, *residual(i))
    for c in range(NB):
        ext_ref[EXT * c : EXT * (c + 1), :] = total[:, c * LANES : (c + 1) * LANES]
    ext_ref[EXT * NB :, :] = jnp.zeros((EXT_ROWS - EXT * NB, LANES), F32)


def panel(place, mine, other, diag, rhs, samples, prev_t):
    vec = pl.BlockSpec((1, ROWS), whole)
    return pl.pallas_call(
        panel_kernel,
        grid=(1,),
        out_shape=(jax.ShapeDtypeStruct((PANEL, ROWS), F32), jax.ShapeDtypeStruct((EXT_ROWS, LANES), F32)),
        in_specs=[
            pl.BlockSpec(memory_space=pltpu.SMEM),
            pl.BlockSpec((HALF, LANES), whole),
            pl.BlockSpec((HALF, LANES), whole),
            vec,
            vec,
            pl.BlockSpec(memory_space=pl.ANY),
            pl.BlockSpec(memory_space=pl.ANY),
        ],
        out_specs=(pl.BlockSpec((PANEL, ROWS), whole), pl.BlockSpec((EXT_ROWS, LANES), whole)),
        scratch_shapes=[
            pltpu.VMEM((PANEL, FEAT), BF16),
            pltpu.VMEM((2 * PANEL, PREV), BF16),
            pltpu.VMEM((PANEL, LANES), F32),
            pltpu.VMEM((PANEL, PANEL), F32),
            pltpu.VMEM((ROWS, FEAT), BF16),
            pltpu.VMEM((PREV, ROWS), F32),
            pltpu.SemaphoreType.DMA((2, ROWS // PANEL_TILE)),
        ],
        compiler_params=pltpu.CompilerParams(vmem_limit_bytes=VMEM_LIMIT),
        cost_estimate=pl.CostEstimate(flops=2 * ROWS * RANK * 1000, bytes_accessed=ROWS * (FEAT * 2 + PREV * 4), transcendentals=0),
        name="panel",
    )(place, mine, other, diag, rhs, samples, prev_t)


def inverse8(cols):
    sub = lax.broadcasted_iota(jnp.int32, (8, LANES), 0)

    def row(x, r):
        return jnp.broadcast_to(x[r : r + 1, :], (8, LANES))

    cols = list(cols)
    for k in range(0, 8, 2):
        a, b, c = row(cols[k], k), row(cols[k + 1], k), row(cols[k + 1], k + 1)
        scale = 1.0 / (a * c - b * b)
        ia, ib, ic = c * scale, -b * scale, a * scale
        ua = cols[k] * ia + cols[k + 1] * ib
        ub = cols[k] * ib + cols[k + 1] * ic
        keep = (sub != k) & (sub != k + 1)
        first = sub == k
        for m in range(8):
            if m in (k, k + 1):
                continue
            x, y = row(cols[m], k), row(cols[m], k + 1)
            cols[m] = jnp.where(keep, cols[m] - (ua * x + ub * y), jnp.where(first, ia * x + ib * y, ib * x + ic * y))
        cols[k] = jnp.where(keep, -ua, jnp.where(first, ia, ib))
        cols[k + 1] = jnp.where(keep, -ub, jnp.where(first, ib, ic))
    return cols


def tree(terms):
    while len(terms) > 1:
        terms = [a + b for a, b in zip(terms[::2], terms[1::2])]
    return terms[0]


def inverse128(rows):
    lane = lax.broadcasted_iota(jnp.int32, (8, LANES), 1)
    sub = lax.broadcasted_iota(jnp.int32, (8, LANES), 0)
    rows = list(rows)
    n = len(rows)

    def spread(x, at):
        return jnp.broadcast_to(x[:, at : at + 1], (8, LANES))

    for p in range(n):
        inside = (lane >= 8 * p) & (lane < 8 * p + 8)
        cols = inverse8([spread(rows[p], 8 * p + j) for j in range(8)])
        own = jnp.where(inside, jnp.where(lane == sub + 8 * p, 1.0, 0.0), rows[p])
        pivot = tree([cols[j] * jnp.broadcast_to(own[j : j + 1, :], (8, LANES)) for j in range(8)])
        times = jnp.where(inside, 0.0, jnp.where(lane < 8 * p, -rows[p], rows[p]))
        if p + 1 < n:
            update = tree([spread(rows[p + 1], 8 * p + j) * jnp.broadcast_to(pivot[j : j + 1, :], (8, LANES)) for j in range(8)])
            following = jnp.where(inside, 0.0, rows[p + 1]) - update
        h, m, lo = (x.astype(F32) for x in three(times))
        ph, pm, plo = (x.astype(F32) for x in three(pivot))
        left = jnp.concatenate([h, h, m, m, h, lo], axis=0).astype(BF16)
        right = jnp.concatenate([ph, pm, ph, pm, plo, ph], axis=0).astype(BF16)
        update = mm(left, right, TN)
        for q in range(n):
            if q not in (p, p + 1):
                rows[q] = jnp.where(inside, 0.0, rows[q]) - update[8 * q : 8 * q + 8]
        rows[p] = pivot
        if p + 1 < n:
            rows[p + 1] = following
        yield
    return rows


EXTRA = EXT - PANEL


def left_parts(x):
    h, m, lo = three(x)
    return jnp.concatenate([h, m], axis=1), jnp.concatenate([h, lo], axis=1)


def right_parts(x, axis):
    h, m, lo = three(x)
    return tuple(jnp.concatenate(pair, axis=axis) for pair in ((h, h), (m, m), (lo, h)))


def product(left, right, dims):
    return mm(left[0], right[0], dims) + (mm(left[0], right[1], dims) + mm(left[1], right[2], dims))


def run(steps, fillers):
    count = LANES // 8
    done = 0
    for i in range(count + 1):
        try:
            next(steps)
        except StopIteration as end:
            for filler in fillers[done:]:
                filler()
            return end.value
        upto = len(fillers) * (i + 1) // count
        for filler in fillers[done:upto]:
            filler()
        done = upto


def eliminate(first, last, cols, t_refs, inv_ref):
    fillers = []
    for k in range(first, last):
        ref, at = cols[k]
        n = PACKED[k] - LANES
        block = run(inverse128([ref[at + 8 * i : at + 8 * i + 8, :] for i in range(LANES // 8)]), fillers)
        block = jnp.concatenate(block, axis=0)
        inv_ref[(k - first) * LANES : (k - first + 1) * LANES, :] = block
        weights = right_parts(block, 0)
        near = min(LANES, n)
        below = ref[at + LANES : at + LANES + near, :]
        right_near = right_parts(below, 1)
        times = product(left_parts(below), weights, NN)
        t_refs[k][:near, :] = times
        next_ref, next_at = cols[k + 1]
        next_ref[next_at : next_at + near, :near] -= product(left_parts(times), right_near, NT)
        fillers = []
        if n == near:
            continue
        far = {}

        def others(ref=ref, at=at, n=n, t_ref=t_refs[k], weights=weights, far=far):
            below = ref[at + 2 * LANES : at + LANES + n, :]
            times = product(left_parts(below), weights, NN)
            t_ref[LANES:, :] = times
            far["left"] = left_parts(times)
            far["right"] = right_parts(below, 1)

        def beside(ref=next_ref, at=next_at, n=n, far=far, right=right_near):
            ref[at + LANES : at + n, :] -= product(far["left"], right, NT)

        def update(j, k=k, n=n, far=far):
            r = (j - k - 2) * LANES
            wide = min(2 * LANES, n - LANES - r)
            value = product(tuple(x[r:] for x in far["left"]), tuple(x[r : r + wide] for x in far["right"]), NT)
            for c in range(0, wide, LANES):
                to_ref, to = cols[j + c // LANES]
                w = min(LANES, wide - c)
                to_ref[to : to + n - LANES - r - c, :w] -= value[c:, c : c + w]

        fillers = [others, beside] + [functools.partial(update, j) for j in range(k + 2, NB, 2)]
    for filler in fillers:
        filler()


CUTS = (0, 4, 7)
LEFT = [PACKED_AT[j] - PACKED_AT[CUTS[1]] for j in range(CUTS[1], NB + 1)]


def solve_first_kernel(place_ref, mine_ref, other_ref, left_ref, inv_ref, token_ref, *refs):
    token_ref[...] = jnp.zeros_like(token_ref)
    t_refs, a_ref = refs[:-1], refs[-1]
    lane = lax.broadcasted_iota(jnp.int32, (LANES, LANES), 1)
    sub = lax.broadcasted_iota(jnp.int32, (LANES, LANES), 0)

    def load(halves):
        for half, at, to, n in by_half(0, PACKED_AT[CUTS[1]]):
            a_ref[to : to + n, :] = halves[half][at : at + n, :]
        for half, at, to, n in by_half(PACKED_AT[CUTS[1]], GRAM_ROWS):
            left_ref[to : to + n, :] = halves[half][at : at + n, :]

    @pl.when(place_ref[1] == 0)
    def _():
        load((mine_ref, other_ref))

    @pl.when(place_ref[1] == 1)
    def _():
        load((other_ref, mine_ref))

    cols = [(a_ref, PACKED_AT[j]) for j in range(CUTS[1])] + [(left_ref, LEFT[j - CUTS[1]]) for j in range(CUTS[1], NB)]
    for j, (ref, at) in enumerate(cols):
        n = min(LANES, PACKED[j])
        ref[at : at + n, :] += jnp.where(lane == sub, 1.0, 0.0)[:n]
    eliminate(0, CUTS[1], cols, dict(enumerate(t_refs)), inv_ref)


def solve_second_kernel(token_ref, left_ref, last_ref, inv_ref, *refs):
    t_refs, a_ref = refs[:-1], refs[-1]
    a_ref[...] = left_ref[...]
    eliminate(CUTS[1], CUTS[2], {j: (a_ref, LEFT[j - CUTS[1]]) for j in range(CUTS[1], NB)}, {CUTS[1] + i: r for i, r in enumerate(t_refs)}, inv_ref)
    last_ref[...] = a_ref[LEFT[-2] :, :]


def solve_last_kernel(last_ref, inv0_ref, inv1_ref, ext_ref, diag_ref, rhs_ref, new_ref, prev_any, *refs):
    t_refs, (out_ref, e_ref, w_ref, prev_ref, sem) = refs[: NB - 1], refs[NB - 1 :]
    step = PREV // 4
    copies = [pltpu.make_async_copy(prev_any.at[pl.ds(i * step, step)], prev_ref.at[pl.ds(i * step, step)], sem.at[i]) for i in range(4)]
    for copy in copies:
        copy.start()
    tail = PREV % LANES
    for j in range(NB):
        e_ref[:, j * LANES : (j + 1) * LANES] = ext_ref[EXT * j : EXT * (j + 1), :]
    scaled = []
    for k in range(NB - 1):
        here = e_ref[:, k * LANES : (k + 1) * LANES]
        left = left_parts(here)
        n = PACKED[k] - LANES
        change = product(left, right_parts(t_refs[k][...], 1), NT)
        e_ref[:, (k + 1) * LANES : PREV] -= change
        inv = inv0_ref[k * LANES : (k + 1) * LANES, :] if k < CUTS[1] else inv1_ref[(k - CUTS[1]) * LANES : (k - CUTS[1] + 1) * LANES, :]
        times = product(left, right_parts(inv, 0), NN)
        scaled.append(times)
        corner = product(left, right_parts(times, 1), NT)
        total = corner if k == 0 else total + corner
    lane = lax.broadcasted_iota(jnp.int32, (LANES, LANES), 1)
    sub = lax.broadcasted_iota(jnp.int32, (LANES, LANES), 0)
    shifted = jnp.concatenate([jnp.zeros((EXT, tail), F32), total[:, :PANEL]], axis=1)
    bottom = e_ref[:, (NB - 1) * LANES :] - shifted
    bottom = bottom + jnp.where(lax.broadcasted_iota(jnp.int32, (EXT, LANES), 1) == lax.broadcasted_iota(jnp.int32, (EXT, LANES), 0) + tail, 1.0, 0.0)
    block = jnp.concatenate([last_ref[...], bottom[:PANEL]], axis=0)
    block = jnp.where((lane >= tail) & (sub < tail), block.T, block)
    inverse = run(inverse128([block[8 * i : 8 * i + 8, :] for i in range(LANES // 8)]), [])
    inverse = jnp.concatenate(inverse, axis=0)
    value = mm(bottom[PANEL:], inverse, NN, HIGHEST)
    sums = [None] * (NB - 1)
    for k in reversed(range(1, NB)):
        spread = column(value[:1])
        w_ref[k * LANES : (k + 1) * LANES, :] = spread
        for j in range(k):
            r = (k - j - 1) * LANES
            rows = t_refs[j][r : r + min(LANES, PREV - k * LANES), :]
            if k == NB - 1:
                rows = jnp.concatenate([rows, scaled[j][:PANEL]], axis=0)
            part = (rows * spread).reshape(LANES // 8, 8, LANES).sum(axis=0)
            sums[j] = part if sums[j] is None else sums[j] + part
        value = scaled[k - 1][PANEL:] - jnp.sum(sums[k - 1], axis=0, keepdims=True)


    w_ref[:LANES, :] = column(value[:1])

    def weigh(ref, at, to):
        return ref[pl.ds(at, 8), :] * jnp.concatenate([w_ref[pl.ds(to, 8), :]] * (ROWS // LANES), axis=1)

    total = tree([weigh(new_ref, 8 * i, PREV + 8 * i) for i in range(PANEL // 8)])
    for copy in copies:
        copy.wait()

    for i in range(0, PREV, 32):
        total = total + tree([weigh(prev_ref, i + 8 * j, i + 8 * j) for j in range(4)])
    fw = jnp.sum(total, axis=0, keepdims=True)
    out_ref[...] = diag_ref[...] * rhs_ref[...] - diag_ref[...] * fw


def block_spec(rows):
    return pl.BlockSpec((rows, LANES), whole)


def shape(rows):
    return jax.ShapeDtypeStruct((rows, LANES), F32)


def solve_first(place, mine, other):
    below = [PACKED[k] - LANES for k in range(CUTS[1])]
    outs = [LEFT[-1], CUTS[1] * LANES, 8] + below
    return pl.pallas_call(
        solve_first_kernel,
        grid=(1,),
        out_shape=tuple(shape(r) for r in outs),
        in_specs=[pl.BlockSpec(memory_space=pltpu.SMEM), block_spec(HALF), block_spec(HALF)],
        out_specs=tuple(block_spec(r) for r in outs),
        scratch_shapes=[pltpu.VMEM((PACKED_AT[CUTS[1]], LANES), F32)],
        compiler_params=pltpu.CompilerParams(vmem_limit_bytes=VMEM_LIMIT),
        cost_estimate=pl.CostEstimate(flops=2 * 10**10, bytes_accessed=10**7, transcendentals=0),
        name="solve_first",
    )(place, mine, other)


def solve_second(token, left):
    below = [PACKED[k] - LANES for k in range(CUTS[1], CUTS[2])]
    outs = [PACKED[NB - 1], (CUTS[2] - CUTS[1]) * LANES] + below
    return pl.pallas_call(
        solve_second_kernel,
        grid=(1,),
        out_shape=tuple(shape(r) for r in outs),
        in_specs=[pl.BlockSpec(memory_space=pl.ANY), block_spec(LEFT[-1])],
        out_specs=tuple(block_spec(r) for r in outs),
        scratch_shapes=[pltpu.VMEM((LEFT[-1], LANES), F32)],
        compiler_params=pltpu.CompilerParams(vmem_limit_bytes=VMEM_LIMIT),
        cost_estimate=pl.CostEstimate(flops=2 * 10**10, bytes_accessed=10**7, transcendentals=0),
        name="solve_second",
    )(token, left)


def solve_last(last, inv0, inv1, ext, t, diag, rhs, new_t, prev_t):
    ins = [PACKED[NB - 1], CUTS[1] * LANES, (CUTS[2] - CUTS[1]) * LANES, EXT_ROWS]
    below = [PACKED[k] - LANES for k in range(NB - 1)]
    vec = pl.BlockSpec((1, ROWS), whole)
    return pl.pallas_call(
        solve_last_kernel,
        grid=(1,),
        out_shape=jax.ShapeDtypeStruct((1, ROWS), F32),
        in_specs=[block_spec(r) for r in ins]
        + [vec, vec, pl.BlockSpec((PANEL, ROWS), whole), pl.BlockSpec(memory_space=pl.ANY)]
        + [block_spec(r) for r in below],
        out_specs=vec,
        scratch_shapes=[
            pltpu.VMEM((EXT, RANK), F32),
            pltpu.VMEM((RANK, LANES), F32),
            pltpu.VMEM((PREV, ROWS), F32),
            pltpu.SemaphoreType.DMA((4,)),
        ],
        compiler_params=pltpu.CompilerParams(vmem_limit_bytes=VMEM_LIMIT),
        name="solve_last",
    )(last, inv0, inv1, ext, diag, rhs, new_t, prev_t, *t)


SAME_CORE = [[i for i in range(128) if i % 2 == core] for core in range(2)]
OTHER_CORE = [(i, i ^ 1) for i in range(128)]


def sum_large(keep, send):
    shape = keep.shape
    keep = (keep + lax.ppermute(send, AXES, OTHER_CORE)).reshape(64, -1, LANES)
    parts = lax.all_to_all(keep, AXES, 0, 0, axis_index_groups=SAME_CORE)
    part = jnp.sum(parts, axis=0)
    mine = lax.all_to_all(jnp.broadcast_to(part, parts.shape), AXES, 0, 0, axis_index_groups=SAME_CORE)
    mine = mine.reshape(shape)
    return mine, lax.ppermute(mine, AXES, OTHER_CORE)


def on_device(samples, prev_factor, pivots, inv_diag, rhs):
    index = lax.axis_index(AXES)
    place = jnp.concatenate([jnp.stack([index, index % 2]), pivots - index * ROWS]).astype(jnp.int32)
    diag, rhs = inv_diag.reshape(1, ROWS), rhs.reshape(1, ROWS)
    prev_t = prev_factor.T
    keep, send = gram(samples, prev_t, diag, place)
    mine, other = sum_large(keep, send)
    new_t, ext = panel(place, mine, other, diag, rhs, samples, prev_t)
    parts = lax.all_to_all(ext.reshape(128, -1, LANES), AXES, 0, 0)
    left, inv0, token, *t0 = solve_first(place, mine, other)
    parts, token = lax.optimization_barrier((parts, token))
    part = jnp.sum(parts, axis=0)
    ext = lax.all_to_all(jnp.broadcast_to(part, parts.shape), AXES, 0, 0).reshape(ext.shape)
    last, inv1, *t1 = solve_second(token, left)
    out = solve_last(last, inv0, inv1, ext, t0 + t1, diag, rhs, new_t, prev_t)
    return (new_t.T, out.reshape(ROWS))


def solution(mesh):
    return jax.shard_map(
        on_device,
        mesh=mesh,
        in_specs=(
            P(AXES, None),
            P(AXES, None),
            P(),
            P(AXES),
            P(AXES),
        ),
        out_specs=(P(AXES, None), P(AXES)),
        check_vma=False,
    )
```
